128 devices in a mesh: gx: 8 (over y, core), gy: 16 (over z, x).
Axes of the slice: x: 4, y: 4, z: 4, core: 2. Of those that a mesh axis runs over, the one named last changes fastest.
Arguments:
- adjoint_final: float32 [19, 256, 32768], P(None, 'gx', 'gy'), may hold values from -6 to 6
- base_velocity: float32 [2, 3, 256, 32768], P(None, None, 'gx', 'gy'), may hold values from -0.25 to 0.25
- base_density: float32 [2, 256, 32768], P(None, 'gx', 'gy'), may hold values from 0.8 to 1.2
- heights: int32 [256, 512], P('gx', 'gy'), may hold values from 0 to 32, as said below
- sensor_cells: int32 [8, 16, 128], P('gx', 'gy'), may hold values from 0 to 65535
- sensor_misfit: float32 [2, 3, 8, 16, 128], P(None, None, 'gx', 'gy'), may hold values from -8 to 8
Outputs:
- adjoint_start: float32 [19, 256, 32768], P(None, 'gx', 'gy')
The draws below stay inside these ranges and needn't reach their ends.
Inputs may be any that keep to these rules, and one draw needn't show every extreme that they name: `heights`: buildings stand on lots of 6 x 6 columns in a grid of 8 x 8 columns (streets have height 0); some lots are empty.
All inputs are finite; a program needn't handle non-finite values.
Results may differ from the reference program's by a relative error of at most 0.0003.
Values sent between devices are 32-bit elements; how exact they have to be, the bound alone decides.
No kernel may reach another device: no remote copies, remote signals or barrier semaphores. Data moves between devices by JAX's collectives and lax.ppermute only.
A program may use at most 192 MiB of HBM per device.

```python
import jax
import jax.numpy as jnp

LINKS = 19
CX = 32
CY = 32
NZ = 64
STEPS = 2
SENS = 128
PX = 8
PY = 16
NX = 256
NY = 512


def draw_heights(key, part):
    lot_keys = jax.random.split(jax.random.fold_in(key, 7), 2)
    blocks_x = NX // 8 + 1
    blocks_y = NY // 8 + 1
    tallness = jax.random.randint(lot_keys[0], (blocks_x, blocks_y), 1, NZ // 2 + 1)
    occupied = jax.random.randint(lot_keys[1], (blocks_x, blocks_y), 0, 4) > 0
    block_height = jnp.where(occupied, tallness, 0)
    along_x = jnp.arange(NX, dtype=jnp.int32)
    along_y = jnp.arange(NY, dtype=jnp.int32)
    spread = block_height[along_x // 8][:, along_y // 8]
    inside = (along_x % 8 < 6)[:, None] & (along_y % 8 < 6)[None, :]
    return jnp.where(inside, spread, 0).astype(jnp.int32)


def plant(result, key, low, top_value):
    longest = result.shape.index(max(result.shape))
    spots = []
    for shift in (0, 1):
        where = [jax.random.randint(jax.random.fold_in(key, axis), (), 0, length) for axis, length in enumerate(result.shape)]
        where[longest] = (where[longest] + shift) % result.shape[longest]
        spots.append(tuple(where))
    return result.at[spots[0]].set(low).at[spots[1]].set(top_value)


def level_of(own_key, dims, cuts, low, top_value):
    def one(position, shards_of):
        steps = jax.random.uniform(jax.random.fold_in(jax.random.fold_in(own_key, 6), position), (shards_of,), jnp.float32, low / len(cuts), top_value / len(cuts))
        return jnp.repeat(jnp.exp(steps), dims[position] // shards_of).reshape((-1,) + (1,) * (len(dims) - position - 1))

    gain = one(*cuts[0])
    for cut in cuts[1:]:
        gain = gain * one(*cut)
    return gain


def gaussian(stream_key, shape, scale, most, cuts=(), kind=jnp.bfloat16):
    level = level_of(stream_key, shape, cuts, -0.22, 0.18) if cuts else 1.0
    entries = jax.random.normal(stream_key, shape, jnp.float32) * scale * level
    return jnp.minimum(jnp.maximum(entries, -most), most).astype(kind)


def setup_inputs(seed: int = 0) -> dict:
    splits = jax.random.split(jax.random.key(seed), 7)
    return {
        "adjoint_final": gaussian(splits[0], (LINKS, NX, NY * NZ), 1.0, 6.0, ((1, 8), (2, 16)), jnp.float32),
        "base_velocity": gaussian(splits[1], (STEPS, 3, NX, NY * NZ), 0.08, 0.25, ((2, 8), (3, 16)), jnp.float32),
        "base_density": jnp.clip(0.8 + 0.40000004 * jax.random.uniform(splits[2], (STEPS, NX, NY * NZ), jnp.float32) ** level_of(splits[2], (STEPS, NX, NY * NZ), ((1, 8), (2, 16)), -0.2, 0.2), 0.8, 1.2),
        "heights": draw_heights(jax.random.fold_in(splits[6], 71), 0),
        "sensor_cells": plant(jax.random.randint(splits[4], (PX, PY, SENS), 0, CX * CY * NZ), jax.random.fold_in(splits[4], 1), 0, (CX * CY * NZ) - 1).astype(jnp.int32),
        "sensor_misfit": gaussian(splits[5], (STEPS, 3, PX, PY, SENS), 2.0, 8.0, ((2, 8), (3, 16)), jnp.float32),
    }


VELOCITIES = ((0, 0, 0), (1, 0, 0), (-1, 0, 0), (0, 1, 0), (0, -1, 0), (0, 0, 1), (0, 0, -1), (1, 1, 0), (-1, -1, 0), (1, -1, 0), (-1, 1, 0), (1, 0, 1), (-1, 0, -1), (1, 0, -1), (-1, 0, 1), (0, 1, 1), (0, -1, -1), (0, 1, -1), (0, -1, 1))
WEIGHTS = (1.0 / 3.0,) + (1.0 / 18.0,) * 6 + (1.0 / 36.0,) * 12
OPPOSITE = (0, 2, 1, 4, 3, 6, 5, 8, 7, 10, 9, 12, 11, 14, 13, 16, 15, 18, 17)
relax_rate = 1.8


def pull_value(source, shift_x, shift_y, shift_z):
    rolled = jnp.roll(source, (-shift_x, -shift_y), axis=(0, 1))
    padded = jnp.pad(rolled, ((0, 0), (0, 0), (1, 1)))
    return padded[:, :, 1 + shift_z:1 + shift_z + NZ]


def collide_back(incoming_at, velocity):
    speed_sq = velocity[0] * velocity[0] + velocity[1] * velocity[1] + velocity[2] * velocity[2]
    blank_field = jnp.zeros_like(velocity[0])
    total_plain = blank_field
    total_square = blank_field
    total_dir = [blank_field, blank_field, blank_field]
    total_mixed = [blank_field, blank_field, blank_field]
    for number in range(19):
        vector = VELOCITIES[number]
        weighted = WEIGHTS[number] * incoming_at(number)
        projection = vector[0] * velocity[0] + vector[1] * velocity[1] + vector[2] * velocity[2]
        total_plain = total_plain + weighted
        total_square = total_square + weighted * projection * projection
        for axis_number in range(3):
            if vector[axis_number] != 0:
                total_dir[axis_number] = total_dir[axis_number] + vector[axis_number] * weighted
                total_mixed[axis_number] = total_mixed[axis_number] + vector[axis_number] * weighted * projection
    scalar_part = total_plain * (1.0 + 1.5 * speed_sq) - 4.5 * total_square
    vector_part = [3.0 * total_dir[axis_number] + 9.0 * total_mixed[axis_number] - 3.0 * velocity[axis_number] * total_plain for axis_number in range(3)]
    collided = []
    for number in range(19):
        vector = VELOCITIES[number]
        along = scalar_part
        for axis_number in range(3):
            if vector[axis_number] != 0:
                along = along + vector[axis_number] * vector_part[axis_number]
        collided.append((1.0 - relax_rate) * incoming_at(number) + relax_rate * along)
    return jnp.stack(collided)


def sensor_forcing(velocity_at, density_at, misfit):
    drift_term = velocity_at[0] * misfit[0] + velocity_at[1] * misfit[1] + velocity_at[2] * misfit[2]
    row_list = []
    for number in range(19):
        vector = VELOCITIES[number]
        along = vector[0] * misfit[0] + vector[1] * misfit[1] + vector[2] * misfit[2]
        row_list.append((along - drift_term) / density_at)
    return jnp.stack(row_list)


def reference(adjoint_final, base_velocity, base_density, heights, sensor_cells, sensor_misfit):
    levels = jnp.arange(NZ, dtype=jnp.int32)
    fluid_mask = (levels[None, None, :] >= heights[:, :, None]).astype(jnp.float32)
    blocked = []
    for number in range(19):
        shift_x, shift_y, shift_z = VELOCITIES[number]
        column_tops = jnp.roll(heights, (-shift_x, -shift_y), axis=(0, 1))
        raised = levels + shift_z
        blocked.append((raised[None, None, :] < column_tops[:, :, None]) | (raised[None, None, :] >= NZ))
    block_x = jnp.arange(PX, dtype=jnp.int32)[:, None, None]
    block_y = jnp.arange(PY, dtype=jnp.int32)[None, :, None]
    within = sensor_cells % (CY * NZ)
    cell_x = (block_x * CX + sensor_cells // (CY * NZ)).reshape(-1)
    cell_y = (block_y * CY + within // NZ).reshape(-1)
    cell_z = (within % NZ).reshape(-1)
    adjoint = adjoint_final.reshape(19, NX, NY, NZ)
    for backward in range(STEPS - 1, -1, -1):
        velocity = base_velocity[backward].reshape(3, NX, NY, NZ)
        density = base_density[backward].reshape(NX, NY, NZ)
        current = adjoint

        def incoming_at(number):
            shift_x, shift_y, shift_z = VELOCITIES[number]
            pulled = pull_value(current[number], shift_x, shift_y, shift_z)
            return jnp.where(blocked[number], current[OPPOSITE[number]], pulled)

        collided = collide_back(incoming_at, velocity)
        misfit = sensor_misfit[backward].reshape(3, -1)
        forcing = sensor_forcing(velocity[:, cell_x, cell_y, cell_z], density[cell_x, cell_y, cell_z], misfit)
        collided = collided.at[:, cell_x, cell_y, cell_z].add(forcing)
        adjoint = collided * fluid_mask
    return adjoint.reshape(19, NX, NY * NZ)
```

```python
import functools

import jax
import jax.numpy as jnp
from jax import lax
from jax.experimental import pallas as pl
from jax.experimental.pallas import tpu as pltpu
from jax.sharding import PartitionSpec as P

VELOCITIES = (
    (0, 0, 0),
    (1, 0, 0),
    (-1, 0, 0),
    (0, 1, 0),
    (0, -1, 0),
    (0, 0, 1),
    (0, 0, -1),
    (1, 1, 0),
    (-1, -1, 0),
    (1, -1, 0),
    (-1, 1, 0),
    (1, 0, 1),
    (-1, 0, -1),
    (1, 0, -1),
    (-1, 0, 1),
    (0, 1, 1),
    (0, -1, -1),
    (0, 1, -1),
    (0, -1, 1),
)
OPPOSITE = (0, 2, 1, 4, 3, 6, 5, 8, 7, 10, 9, 12, 11, 14, 13, 16, 15, 18, 17)
K = 19
ROWS, COLS, NZ = 32, 32, 64
TILES = COLS * NZ // 128
EXT = 48
BASE = 8
SENS = 128
STARTS_WIDE = (7, 15, 23, 31, 33)
STARTS_OWN = (8, 16, 24, 32)
X_SIDE = {"lo": (1, 7, 9, 11, 13), "hi": (2, 8, 10, 12, 14)}
Y_SIDE = {"lo": (3, 7, 10, 15, 17), "hi": (4, 8, 9, 16, 18)}
X_FIELDS = 32
Y_FIELDS = 7
F32 = jnp.float32
MB = 1024 * 1024
HBM = pl.BlockSpec(memory_space=pltpu.HBM)
VMEM = pl.BlockSpec(memory_space=pltpu.VMEM)


def add(a, b):
    if a is None:
        return b
    return a if b is None else a + b


def sub(a, b):
    if b is None:
        return a
    return -b if a is None else a - b


def lanes():
    return lax.broadcasted_iota(jnp.int32, (8, 128), 1)


class Geometry:
    def __init__(self):
        lane = lanes()
        level = lane % NZ
        self.low = lane < NZ
        self.level = level.astype(F32)
        up = jnp.where(level == NZ - 1, -1, level + 1).astype(F32)
        self.raised = {0: self.level, 1: up, -1: self.level - 1.0}


def half_turn(value):
    return pltpu.roll(value, NZ, 1)


def from_next(geo, here, after):
    return jnp.where(geo.low, after, here)


def from_previous(geo, here, before):
    return jnp.where(geo.low, here, before)


def pull(geo, read, tile, after, before, position, number):
    cx, cy, cz = VELOCITIES[number]
    row = position + cx
    if cy == 0:
        value = read(tile, number, row)
        return pltpu.roll(value, (128 - cz) % 128, 1) if cz else value
    if cy == 1:
        value = from_next(geo, read(tile, number, row), read(after, number, row))
    else:
        value = from_previous(geo, read(tile, number, row), read(before, number, row))
    return pltpu.roll(value, NZ - cz, 1)


def incoming(geo, read, tops, tile, after, before, position, numbers):
    out = [None] * K
    for number in numbers:
        cx, cy, cz = VELOCITIES[number]
        value = pull(geo, read, tile, after, before, position, number)
        if number:
            blocked = geo.raised[cz] < tops(cy, position + cx)
            value = jnp.where(blocked, read(tile, OPPOSITE[number], position), value)
        out[number] = value
    return out


def moments(f):
    plus = [None] * K
    minus = [None] * K
    for number in range(1, K, 2):
        plus[number] = add(f[number], f[number + 1])
        minus[number] = sub(f[number], f[number + 1])
    sxy, dxy = add(plus[7], plus[9]), sub(plus[7], plus[9])
    sxz, dxz = add(plus[11], plus[13]), sub(plus[11], plus[13])
    syz, dyz = add(plus[15], plus[17]), sub(plus[15], plus[17])
    twice = [None if plus[n] is None else plus[n] + plus[n] for n in (1, 3, 5)]
    mxx = add(twice[0], add(sxy, sxz))
    myy = add(twice[1], add(sxy, syz))
    mzz = add(twice[2], add(sxz, syz))
    total = add(add(add(twice[0], twice[1]), twice[2]), add(add(sxy, sxz), syz))
    if f[0] is not None:
        total = add(12.0 * f[0], total)

    def axis(main, first, second):
        doubled = None if minus[main] is None else minus[main] + minus[main]
        return add(doubled, add(first, second))

    jx = axis(1, add(minus[7], minus[9]), add(minus[11], minus[13]))
    jy = axis(3, sub(minus[7], minus[9]), add(minus[15], minus[17]))
    jz = axis(5, sub(minus[11], minus[13]), sub(minus[15], minus[17]))
    return total, (jx, jy, jz), (mxx, myy, mzz, dxy, dxz, dyz)


def mul(a, b):
    return None if a is None else a * b


def collide(f, u, force, numbers, fluid):
    total, (jx, jy, jz), (mxx, myy, mzz, dxy, dxz, dyz) = moments(f)
    ux, uy, uz = u
    qx = add(add(mul(mxx, ux), mul(dxy, uy)), mul(dxz, uz))
    qy = add(add(mul(dxy, ux), mul(myy, uy)), mul(dyz, uz))
    qz = add(add(mul(dxz, ux), mul(dyz, uy)), mul(mzz, uz))
    speed = ux * ux + uy * uy + uz * uz
    scalar = total * (0.05 + 0.075 * speed) - 0.225 * (ux * qx + uy * qy + uz * qz)
    scaled = 0.15 * total
    vector = []
    for axis, (j, q) in enumerate(((jx, qx), (jy, qy), (jz, qz))):
        vector.append(sub(0.15 * add(j, 3.0 * q), scaled * u[axis]))
    if force is not None:
        scalar = scalar - (ux * force[0] + uy * force[1] + uz * force[2])
        vector = [vector[axis] + force[axis] for axis in range(3)]
    out = {}
    along = {}
    for number in numbers:
        c = VELOCITIES[number]
        pair = number if number % 2 else number - 1
        if number == 0:
            value = scalar
        else:
            if pair not in along:
                first = VELOCITIES[pair]
                cv = None
                for axis in range(3):
                    if first[axis] == 1:
                        cv = add(cv, vector[axis])
                    elif first[axis] == -1:
                        cv = sub(cv, vector[axis])
                along[pair] = cv
            value = scalar + along[pair] if number == pair else scalar - along[pair]
        if f[number] is not None:
            value = value - 0.8 * f[number]
        out[number] = jnp.where(fluid, value, 0.0)
    return out


def split3(value):
    high = value.astype(jnp.bfloat16)
    rest = value - high.astype(F32)
    middle = rest.astype(jnp.bfloat16)
    low = (rest - middle.astype(F32)).astype(jnp.bfloat16)
    return high, middle, low


def sensor_rows(position, misfit):
    count = position.shape[-1]
    rows = lax.broadcasted_iota(jnp.int32, (EXT, count), 0)
    here = rows == position
    parts = []
    for axis in range(3):
        parts.extend(split3(jnp.where(here, misfit[axis], 0.0)))
    return jnp.concatenate(parts, axis=0)


def sensor_field(left, lane, tile):
    count = lane.shape[-1]
    cells = lax.broadcasted_iota(jnp.int32, (128, count), 0) + tile * 128
    right = jnp.where(cells == lane, 1.0, 0.0).astype(jnp.bfloat16)
    product = lax.dot_general(
        left, right, (((1,), (1,)), ((), ())), preferred_element_type=F32
    )
    field = []
    for axis in range(3):
        parts = [product[(3 * axis + part) * EXT : (3 * axis + part + 1) * EXT] for part in range(3)]
        field.append(parts[0] + (parts[1] + parts[2]))
    return field


def by_parity(parity, even, odd):
    pl.when(parity == 0)(even)
    pl.when(parity == 1)(odd)


def pack_x_kernel(parity_ref, adjoint, velocity, density, heights, cells, misfit, out_a, out_b,
                  rows_buf, u_buf, rho_buf, sems):
    copies = []
    for side, start in ((0, 0), (1, ROWS - 8)):
        for tile in range(TILES):
            at = pl.ds(tile * 128, 128)
            copies.append(
                pltpu.make_async_copy(adjoint.at[:, pl.ds(start, 8), at], rows_buf.at[side, tile], sems.at[side, tile])
            )
        copies.append(pltpu.make_async_copy(velocity.at[1, :, pl.ds(start, 8), :], u_buf.at[side], sems.at[side, TILES]))
        copies.append(pltpu.make_async_copy(density.at[1, pl.ds(start, 8), :], rho_buf.at[side], sems.at[side, TILES + 1]))
    for copy in copies:
        copy.start()
    for copy in copies:
        copy.wait()
    flat = rows_buf.reshape(2, TILES, K * 8, 128)

    def pack(side, out):
        slot = 0 if side == "lo" else 1
        first = 0 if side == "lo" else 7
        second = 1 if side == "lo" else 6
        for tile in range(TILES):
            at = pl.ds(tile * 128, 128)
            out[0:8, at] = flat[slot, tile, pl.ds(first, 8, stride=8), :]
            out[8:16, at] = flat[slot, tile, pl.ds(64 + first, 8, stride=8), :]
            out[16:19, at] = flat[slot, tile, pl.ds(128 + first, 3, stride=8), :]
            for index, number in enumerate(X_SIDE[side]):
                out[19 + index : 20 + index, at] = rows_buf[slot, tile, number, second : second + 1, :]
        for axis in range(3):
            out[24 + axis : 25 + axis, :] = u_buf[slot, axis, first : first + 1, :]
        out[27:28, :] = rho_buf[slot, first : first + 1, :]
        edge = 0 if side == "lo" else ROWS - 1
        inner = 1 if side == "lo" else ROWS - 2
        out[28:29, 0:COLS] = heights[edge : edge + 1, :].astype(F32)
        out[28:29, 128 : 128 + COLS] = heights[inner : inner + 1, :].astype(F32)
        out[28:29, 256:384] = cells[0].astype(F32)
        for axis in range(3):
            out[28:29, 384 + 128 * axis : 512 + 128 * axis] = misfit[1, axis, 0]

    def even():
        pack("hi", out_a)
        pack("lo", out_b)

    def odd():
        pack("lo", out_a)
        pack("hi", out_b)

    by_parity(parity_ref[0], even, odd)


def pack_x(parity, adjoint, velocity, density, heights, cells, misfit):
    shape = jax.ShapeDtypeStruct((X_FIELDS, TILES * 128), F32)
    return pl.pallas_call(
        pack_x_kernel,
        out_shape=(shape, shape),
        in_specs=[pl.BlockSpec(memory_space=pltpu.SMEM), HBM, HBM, HBM, VMEM, VMEM, VMEM],
        out_specs=(VMEM, VMEM),
        scratch_shapes=[
            pltpu.VMEM((2, TILES, K, 8, 128), F32),
            pltpu.VMEM((2, 3, 8, TILES * 128), F32),
            pltpu.VMEM((2, 8, TILES * 128), F32),
            pltpu.SemaphoreType.DMA((2, TILES + 2)),
        ],
        compiler_params=pltpu.CompilerParams(vmem_limit_bytes=16 * MB),
        name="pack_x",
    )(parity, adjoint, velocity, density, heights, cells, misfit)


def place_x(message, side, tiles, field, u, rho, tall):
    outer, inner = (BASE + ROWS, BASE + ROWS + 1) if side == "lo" else (BASE - 1, BASE - 2)
    flat = field.reshape(field.shape[0], K * EXT, 128)
    for slot, tile in tiles:
        at = pl.ds(tile * 128, 128)
        flat[slot, pl.ds(outer, 8, stride=EXT), :] = message[0:8, at]
        flat[slot, pl.ds(8 * EXT + outer, 8, stride=EXT), :] = message[8:16, at]
        flat[slot, pl.ds(16 * EXT + outer, 3, stride=EXT), :] = message[16:19, at]
        for index, number in enumerate(X_SIDE[side]):
            field[slot, number, inner : inner + 1, :] = message[19 + index : 20 + index, at]
        for axis in range(3):
            u[slot, axis, outer : outer + 1, :] = message[24 + axis : 25 + axis, at]
        rho[slot, outer : outer + 1, :] = message[27:28, at]
    tall[outer : outer + 1, 0:COLS] = message[28:29, 0:COLS]
    tall[inner : inner + 1, 0:COLS] = message[28:29, 128 : 128 + COLS]


def column_tops(geo, tall, tile):
    low = lax.broadcasted_iota(jnp.int32, (EXT, 128), 1) < NZ
    left = jnp.broadcast_to(tall[:, 2 * tile : 2 * tile + 1], (EXT, 128))
    right = jnp.broadcast_to(tall[:, 2 * tile + 1 : 2 * tile + 2], (EXT, 128))
    return jnp.where(low, left, right)


def own_sensors(cells, misfit, step):
    numbers = cells[0]
    return (
        numbers // (COLS * NZ) + BASE,
        numbers % (COLS * NZ),
        [misfit[step, axis, 0] for axis in range(3)],
    )


def message_sensors(message, side):
    numbers = message[28:29, 256:384].astype(jnp.int32)
    row = numbers // (COLS * NZ)
    if side == "lo":
        position = jnp.where(row == 0, BASE + ROWS, -1)
    else:
        position = jnp.where(row == ROWS - 1, BASE - 1, -1)
    return (
        position,
        numbers % (COLS * NZ),
        [message[28:29, 384 + 128 * axis : 512 + 128 * axis] for axis in range(3)],
    )


def join_sensors(parts):
    position = jnp.concatenate([part[0] for part in parts], axis=1)
    lane = jnp.concatenate([part[1] for part in parts], axis=1)
    misfit = [jnp.concatenate([part[2][axis] for part in parts], axis=1) for axis in range(3)]
    return position, lane, misfit


def pack_y_kernel(parity_ref, adjoint, velocity, density, heights, cells, misfit, msg_a, msg_b,
                  out_a, out_b, field, u, rho, tall, tops, force, partial, sems):
    slots = ((0, 0), (1, TILES - 1))
    copies = []
    for slot, tile in slots:
        at = pl.ds(tile * 128, 128)
        own = pl.ds(BASE, ROWS)
        copies.append(pltpu.make_async_copy(adjoint.at[:, :, at], field.at[slot, :, own, :], sems.at[slot, 0]))
        copies.append(pltpu.make_async_copy(velocity.at[1, :, :, at], u.at[slot, :, own, :], sems.at[slot, 1]))
        copies.append(pltpu.make_async_copy(density.at[1, :, at], rho.at[slot, own, :], sems.at[slot, 2]))
    for copy in copies:
        copy.start()
    tall[BASE : BASE + ROWS, 0:COLS] = heights[...].astype(F32)
    for copy in copies:
        copy.wait()
    geo = Geometry()
    x_parity = parity_ref[0]

    def from_x(low_msg, high_msg):
        place_x(low_msg, "lo", slots, field, u, rho, tall)
        place_x(high_msg, "hi", slots, field, u, rho, tall)
        position, lane, value = join_sensors(
            [own_sensors(cells, misfit, 1), message_sensors(low_msg, "lo"), message_sensors(high_msg, "hi")]
        )
        left = sensor_rows(position, value)
        for slot, tile in slots:
            for axis, part in enumerate(sensor_field(left, lane, tile)):
                force[slot, axis] = part

    by_parity(x_parity, lambda: from_x(msg_a, msg_b), lambda: from_x(msg_b, msg_a))
    for slot, tile in slots:
        tops[slot, 0] = column_tops(geo, tall, tile)
        for row in range(0, EXT, 8):
            tops[slot, 1, row : row + 8] = half_turn(tops[slot, 0, row : row + 8])

    def read(tile, number, row):
        return field[tile, number, pl.ds(row, 8), :]

    for slot, side in ((0, "lo"), (1, "hi")):
        inward = 1 if side == "lo" else -1
        numbers = [n for n in range(K) if VELOCITIES[n][1] in (0, inward)]
        for start in STARTS_WIDE:
            at = pl.ds(start, 8)

            def top(cy, row, slot=slot):
                return tops[slot, 0 if cy == 0 else 1, pl.ds(row, 8), :]

            f = incoming(geo, read, top, slot, slot, slot, start, numbers)
            inverse = 1.0 / rho[slot, at, :]
            velocity_here = [u[slot, axis, at, :] for axis in range(3)]
            push = [force[slot, axis, at, :] * inverse for axis in range(3)]
            fluid = geo.level >= tops[slot, 0, at, :]
            result = collide(f, velocity_here, push, Y_SIDE[side], fluid)
            for index, number in enumerate(Y_SIDE[side]):
                partial[slot, index, at, :] = result[number]

    def write(side, out):
        slot = 0 if side == "lo" else 1
        for start in range(0, 40, 8):
            at = pl.ds(start + BASE - 2, 8)
            pairs = [
                (field[slot, number, at, :], partial[slot, index, at, :])
                for index, number in enumerate(Y_SIDE[side])
            ]
            pairs.append((u[slot, 0, at, :], u[slot, 1, at, :]))
            pairs.append((u[slot, 2, at, :], tops[slot, 0, at, :]))
            for index, (first, second) in enumerate(pairs):
                turned = half_turn(second)
                if side == "lo":
                    value = jnp.where(geo.low, first, turned)
                else:
                    value = jnp.where(geo.low, turned, first)
                out[index, start : start + 8, :] = value

    def even():
        write("hi", out_a)
        write("lo", out_b)

    def odd():
        write("lo", out_a)
        write("hi", out_b)

    by_parity(parity_ref[1], even, odd)


def pack_y(parity, adjoint, velocity, density, heights, cells, misfit, msg_a, msg_b):
    shape = jax.ShapeDtypeStruct((Y_FIELDS, 40, 128), F32)
    return pl.pallas_call(
        pack_y_kernel,
        out_shape=(shape, shape),
        in_specs=[pl.BlockSpec(memory_space=pltpu.SMEM), HBM, HBM, HBM] + [VMEM] * 5,
        out_specs=(VMEM, VMEM),
        scratch_shapes=[
            pltpu.VMEM((2, K, EXT, 128), F32),
            pltpu.VMEM((2, 3, EXT, 128), F32),
            pltpu.VMEM((2, EXT, 128), F32),
            pltpu.VMEM((EXT, 128), F32),
            pltpu.VMEM((2, 2, EXT, 128), F32),
            pltpu.VMEM((2, 3, EXT, 128), F32),
            pltpu.VMEM((2, 5, EXT, 128), F32),
            pltpu.SemaphoreType.DMA((2, 3)),
        ],
        compiler_params=pltpu.CompilerParams(vmem_limit_bytes=16 * MB),
        name="pack_y",
    )(parity, adjoint, velocity, density, heights, cells, misfit, msg_a, msg_b)


def steps_kernel(parity_ref, adjoint, velocity, density, heights, cells, misfit, xmsg_a, xmsg_b, ymsg_a, ymsg_b,
                 out, field, middle, u1, u0, rho1, rho0, tall, tops, force1, force0, side_partial, side_u,
                 in_sems, out_sems):
    own = pl.ds(BASE, ROWS)

    def fetch(tile):
        at = pl.ds(pl.multiple_of(tile * 128, 128), 128)
        return [
            pltpu.make_async_copy(adjoint.at[:, :, at], field.at[tile, :, own, :], in_sems.at[tile, 0]),
            pltpu.make_async_copy(velocity.at[1, :, :, at], u1.at[tile, :, own, :], in_sems.at[tile, 1]),
            pltpu.make_async_copy(velocity.at[0, :, :, at], u0.at[tile, :, own, :], in_sems.at[tile, 2]),
            pltpu.make_async_copy(density.at[1, :, at], rho1.at[tile, own, :], in_sems.at[tile, 3]),
            pltpu.make_async_copy(density.at[0, :, at], rho0.at[tile, own, :], in_sems.at[tile, 4]),
        ]

    def start(tile, carry):
        for copy in fetch(tile):
            copy.start()
        return carry

    def arrived(tile, carry):
        for copy in fetch(tile):
            copy.wait()
        return carry

    lax.fori_loop(0, TILES, start, 0)
    geo = Geometry()
    tall[BASE : BASE + ROWS, 0:COLS] = heights[...].astype(F32)

    position, lane0, value = own_sensors(cells, misfit, 0)
    left0 = sensor_rows(position, value)

    def forces0(tile, carry):
        for axis, part in enumerate(sensor_field(left0, lane0, tile)):
            force0[tile, axis] = part
        return carry

    lax.fori_loop(0, TILES, forces0, 0)
    lax.fori_loop(0, TILES, arrived, 0)

    def from_x(low_msg, high_msg):
        slots = [(tile, tile) for tile in range(TILES)]
        place_x(low_msg, "lo", slots, field, u1, rho1, tall)
        place_x(high_msg, "hi", slots, field, u1, rho1, tall)
        position, lane1, value = join_sensors(
            [own_sensors(cells, misfit, 1), message_sensors(low_msg, "lo"), message_sensors(high_msg, "hi")]
        )
        left1 = sensor_rows(position, value)

        def forces1(tile, carry):
            for axis, part in enumerate(sensor_field(left1, lane1, tile)):
                force1[tile, axis] = part
            return carry

        lax.fori_loop(0, TILES, forces1, 0)

    by_parity(parity_ref[0], lambda: from_x(xmsg_a, xmsg_b), lambda: from_x(xmsg_b, xmsg_a))

    def from_y(low_msg, high_msg):
        for start in range(0, 40, 8):
            at = pl.ds(start + BASE - 2, 8)
            for index in range(Y_FIELDS):
                low_value = low_msg[index, start : start + 8, :]
                high_value = high_msg[index, start : start + 8, :]
                low_turned, high_turned = half_turn(low_value), half_turn(high_value)
                if index < 5:
                    field[TILES, Y_SIDE["lo"][index], at, :] = low_value
                    field[TILES, Y_SIDE["hi"][index], at, :] = high_value
                    side_partial[0, index, at, :] = low_turned
                    side_partial[1, index, at, :] = high_turned
                else:
                    first = jnp.where(geo.low, low_value, high_value)
                    second = jnp.where(geo.low, low_turned, high_turned)
                    if index == 5:
                        side_u[0, at, :] = first
                        side_u[1, at, :] = second
                    else:
                        side_u[2, at, :] = first
                        tops[0, TILES, at, :] = second

    by_parity(parity_ref[1], lambda: from_y(ymsg_a, ymsg_b), lambda: from_y(ymsg_b, ymsg_a))

    for tile in range(TILES):
        tops[0, tile] = column_tops(geo, tall, tile)
    for tile in range(TILES + 1):
        after, before = (tile + 1) % (TILES + 1), (tile - 1) % (TILES + 1)
        for row in range(0, EXT, 8):
            at = pl.ds(row, 8)
            here = tops[0, tile, at, :]
            tops[1, tile, at, :] = half_turn(from_next(geo, here, tops[0, after, at, :]))
            tops[2, tile, at, :] = half_turn(from_previous(geo, here, tops[0, before, at, :]))

    def step(source, target, u, rho, force, starts, tile):
        after = tile + 1
        before = jnp.where(tile == 0, TILES, tile - 1)

        def read(where, number, row):
            return source[where, number, pl.ds(row, 8), :]

        def top(cy, row):
            return tops[cy % 3, tile, pl.ds(row, 8), :]

        for start in starts:
            at = pl.ds(start, 8)
            f = incoming(geo, read, top, tile, after, before, start, range(K))
            inverse = 1.0 / rho[tile, at, :]
            velocity_here = [u[tile, axis, at, :] for axis in range(3)]
            push = [force[tile, axis, at, :] * inverse for axis in range(3)]
            fluid = geo.level >= tops[0, tile, at, :]
            result = collide(f, velocity_here, push, range(K), fluid)
            for number in range(K):
                target[tile, number, at, :] = result[number]

    def first_step(tile, carry):
        step(field, middle, u1, rho1, force1, STARTS_WIDE, tile)
        return carry

    lax.fori_loop(0, TILES, first_step, 0)

    def read_first(where, number, row):
        return field[where, number, pl.ds(row, 8), :]

    for slot, side, other in ((0, "lo", "hi"), (1, "hi", "lo")):
        for start in STARTS_WIDE:
            at = pl.ds(start, 8)

            def top(cy, row):
                return tops[cy % 3, TILES, pl.ds(row, 8), :]

            f = incoming(geo, read_first, top, TILES, 0, TILES - 1, start, Y_SIDE[other])
            velocity_here = [side_u[axis, at, :] for axis in range(3)]
            fluid = geo.level >= tops[0, TILES, at, :]
            result = collide(f, velocity_here, None, Y_SIDE[side], fluid)
            for index, number in enumerate(Y_SIDE[side]):
                middle[TILES, number, at, :] = result[number] + side_partial[slot, index, at, :]

    def send_out(tile):
        at = pl.ds(pl.multiple_of(tile * 128, 128), 128)
        return pltpu.make_async_copy(field.at[tile, :, own, :], out.at[:, :, at], out_sems.at[tile])

    def second_step(tile, carry):
        step(middle, field, u0, rho0, force0, STARTS_OWN, tile)
        send_out(tile).start()
        return carry

    lax.fori_loop(0, TILES, second_step, 0)

    def sent(tile, carry):
        send_out(tile).wait()
        return carry

    lax.fori_loop(0, TILES, sent, 0)


def both_steps(parity, adjoint, velocity, density, heights, cells, misfit, xmsg_a, xmsg_b, ymsg_a, ymsg_b):
    wide = TILES + 1
    return pl.pallas_call(
        steps_kernel,
        out_shape=jax.ShapeDtypeStruct(adjoint.shape, F32),
        in_specs=[pl.BlockSpec(memory_space=pltpu.SMEM), HBM, HBM, HBM] + [VMEM] * 7,
        out_specs=HBM,
        scratch_shapes=[
            pltpu.VMEM((wide, K, EXT, 128), F32),
            pltpu.VMEM((wide, K, EXT, 128), F32),
            pltpu.VMEM((TILES, 3, EXT, 128), F32),
            pltpu.VMEM((TILES, 3, EXT, 128), F32),
            pltpu.VMEM((TILES, EXT, 128), F32),
            pltpu.VMEM((TILES, EXT, 128), F32),
            pltpu.VMEM((EXT, 128), F32),
            pltpu.VMEM((3, wide, EXT, 128), F32),
            pltpu.VMEM((TILES, 3, EXT, 128), F32),
            pltpu.VMEM((TILES, 3, EXT, 128), F32),
            pltpu.VMEM((2, 5, EXT, 128), F32),
            pltpu.VMEM((3, EXT, 128), F32),
            pltpu.SemaphoreType.DMA((TILES, 5)),
            pltpu.SemaphoreType.DMA((TILES,)),
        ],
        compiler_params=pltpu.CompilerParams(vmem_limit_bytes=48 * MB),
        name="both_steps",
    )(parity, adjoint, velocity, density, heights, cells, misfit, xmsg_a, xmsg_b, ymsg_a, ymsg_b)


def partners(count, odd):
    if not odd:
        return [(i, i ^ 1) for i in range(count)]
    return [(i, (i - 1) % count if i % 2 == 0 else (i + 1) % count) for i in range(count)]


def swap(value, axis, odd):
    return lax.ppermute(value, axis, partners(lax.axis_size(axis), odd))


def per_device(adjoint, velocity, density, heights, cells, misfit):
    parity = jnp.stack([lax.axis_index("gx") % 2, lax.axis_index("gy") % 2]).astype(jnp.int32)
    args = (parity, adjoint, velocity, density, heights, cells, misfit)
    x_a, x_b = pack_x(*args)
    x_a, x_b = swap(x_a, "gx", False), swap(x_b, "gx", True)
    y_a, y_b = pack_y(*args, x_a, x_b)
    y_a, y_b = swap(y_a, "gy", False), swap(y_b, "gy", True)
    return both_steps(*args, x_a, x_b, y_a, y_b)


def solution(mesh):
    return jax.shard_map(
        per_device,
        mesh=mesh,
        in_specs=(
            P(None, "gx", "gy"),
            P(None, None, "gx", "gy"),
            P(None, "gx", "gy"),
            P("gx", "gy"),
            P("gx", "gy", None),
            P(None, None, "gx", "gy", None),
        ),
        out_specs=P(None, "gx", "gy"),
        check_vma=False,
    )
```

```python
import functools

import jax
import jax.numpy as jnp
from jax import lax
from jax.experimental import pallas as pl
from jax.experimental.pallas import tpu as pltpu
from jax.sharding import PartitionSpec as P

VELOCITIES = (
    (0, 0, 0),
    (1, 0, 0),
    (-1, 0, 0),
    (0, 1, 0),
    (0, -1, 0),
    (0, 0, 1),
    (0, 0, -1),
    (1, 1, 0),
    (-1, -1, 0),
    (1, -1, 0),
    (-1, 1, 0),
    (1, 0, 1),
    (-1, 0, -1),
    (1, 0, -1),
    (-1, 0, 1),
    (0, 1, 1),
    (0, -1, -1),
    (0, 1, -1),
    (0, -1, 1),
)
OPPOSITE = (0, 2, 1, 4, 3, 6, 5, 8, 7, 10, 9, 12, 11, 14, 13, 16, 15, 18, 17)
K = 19
ROWS, COLS, NZ = 32, 32, 64
TILES = COLS * NZ // 128
EXT = 48
BASE = 8
SENS = 128
STARTS_WIDE = (7, 15, 23, 31, 33)
STARTS_OWN = (8, 16, 24, 32)
STARTS_INNER = (9, 17, 25, 31)
STARTS_EDGE = (7, 33)
X_SIDE = {"lo": (1, 7, 9, 11, 13), "hi": (2, 8, 10, 12, 14)}
Y_SIDE = {"lo": (3, 7, 10, 15, 17), "hi": (4, 8, 9, 16, 18)}
X_FIELDS = 32
Y_FIELDS = 7
F32 = jnp.float32
MB = 1024 * 1024
PREPARE_VMEM = 4 * MB
SMALL_VMEM = 4 * MB
HBM = pl.BlockSpec(memory_space=pltpu.HBM)
VMEM = pl.BlockSpec(memory_space=pltpu.VMEM)


def add(a, b):
    if a is None:
        return b
    return a if b is None else a + b


def sub(a, b):
    if b is None:
        return a
    return -b if a is None else a - b


def lanes():
    return lax.broadcasted_iota(jnp.int32, (8, 128), 1)


class Geometry:
    def __init__(self):
        lane = lanes()
        level = lane % NZ
        self.low = lane < NZ
        self.level = level.astype(F32)
        up = jnp.where(level == NZ - 1, -1, level + 1).astype(F32)
        self.raised = {0: self.level, 1: up, -1: self.level - 1.0}


def half_turn(value):
    return pltpu.roll(value, NZ, 1)


def from_next(geo, here, after):
    return jnp.where(geo.low, after, here)


def from_previous(geo, here, before):
    return jnp.where(geo.low, here, before)


def pull(geo, read, tile, after, before, position, number):
    cx, cy, cz = VELOCITIES[number]
    row = position + cx
    if cy == 0:
        value = read(tile, number, row)
        return pltpu.roll(value, (128 - cz) % 128, 1) if cz else value
    if cy == 1:
        value = from_next(geo, read(tile, number, row), read(after, number, row))
    else:
        value = from_previous(geo, read(tile, number, row), read(before, number, row))
    return pltpu.roll(value, NZ - cz, 1)


def incoming(geo, read, tops, tile, after, before, position, numbers):
    out = [None] * K
    for number in numbers:
        cx, cy, cz = VELOCITIES[number]
        value = pull(geo, read, tile, after, before, position, number)
        if number:
            blocked = geo.raised[cz] < tops(cy, position + cx)
            value = jnp.where(blocked, read(tile, OPPOSITE[number], position), value)
        out[number] = value
    return out


def moments(f):
    plus = [None] * K
    minus = [None] * K
    for number in range(1, K, 2):
        plus[number] = add(f[number], f[number + 1])
        minus[number] = sub(f[number], f[number + 1])
    sxy, dxy = add(plus[7], plus[9]), sub(plus[7], plus[9])
    sxz, dxz = add(plus[11], plus[13]), sub(plus[11], plus[13])
    syz, dyz = add(plus[15], plus[17]), sub(plus[15], plus[17])
    twice = [None if plus[n] is None else plus[n] + plus[n] for n in (1, 3, 5)]
    mxx = add(twice[0], add(sxy, sxz))
    myy = add(twice[1], add(sxy, syz))
    mzz = add(twice[2], add(sxz, syz))
    total = add(add(add(twice[0], twice[1]), twice[2]), add(add(sxy, sxz), syz))
    if f[0] is not None:
        total = add(12.0 * f[0], total)

    def axis(main, first, second):
        doubled = None if minus[main] is None else minus[main] + minus[main]
        return add(doubled, add(first, second))

    jx = axis(1, add(minus[7], minus[9]), add(minus[11], minus[13]))
    jy = axis(3, sub(minus[7], minus[9]), add(minus[15], minus[17]))
    jz = axis(5, sub(minus[11], minus[13]), sub(minus[15], minus[17]))
    return total, (jx, jy, jz), (mxx, myy, mzz, dxy, dxz, dyz)


def mul(a, b):
    return None if a is None else a * b


def collide(f, u, force, numbers, fluid):
    total, (jx, jy, jz), (mxx, myy, mzz, dxy, dxz, dyz) = moments(f)
    ux, uy, uz = u
    qx = add(add(mul(mxx, ux), mul(dxy, uy)), mul(dxz, uz))
    qy = add(add(mul(dxy, ux), mul(myy, uy)), mul(dyz, uz))
    qz = add(add(mul(dxz, ux), mul(dyz, uy)), mul(mzz, uz))
    speed = ux * ux + uy * uy + uz * uz
    scalar = total * (0.05 + 0.075 * speed) - 0.225 * (ux * qx + uy * qy + uz * qz)
    scaled = 0.15 * total
    vector = []
    for axis, (j, q) in enumerate(((jx, qx), (jy, qy), (jz, qz))):
        vector.append(sub(0.15 * add(j, 3.0 * q), scaled * u[axis]))
    if force is not None:
        scalar = scalar - (ux * force[0] + uy * force[1] + uz * force[2])
        vector = [vector[axis] + force[axis] for axis in range(3)]
    out = {}
    along = {}
    for number in numbers:
        c = VELOCITIES[number]
        pair = number if number % 2 else number - 1
        if number == 0:
            value = scalar
        else:
            if pair not in along:
                first = VELOCITIES[pair]
                cv = None
                for axis in range(3):
                    if first[axis] == 1:
                        cv = add(cv, vector[axis])
                    elif first[axis] == -1:
                        cv = sub(cv, vector[axis])
                along[pair] = cv
            value = scalar + along[pair] if number == pair else scalar - along[pair]
        if f[number] is not None:
            value = value - 0.8 * f[number]
        out[number] = jnp.where(fluid, value, 0.0)
    return out


def split3(value):
    high = value.astype(jnp.bfloat16)
    rest = value - high.astype(F32)
    middle = rest.astype(jnp.bfloat16)
    low = (rest - middle.astype(F32)).astype(jnp.bfloat16)
    return high, middle, low


def by_parity(parity, even, odd):
    pl.when(parity == 0)(even)
    pl.when(parity == 1)(odd)


def pack_x_kernel(adjoint, velocity, density, heights_hbm, cells_hbm, misfit_hbm, out_a, out_b,
                  rows_buf, u_buf, rho_buf, heights, cells, misfit, sems):
    copies = [
        pltpu.make_async_copy(heights_hbm, heights, sems.at[2, 0]),
        pltpu.make_async_copy(cells_hbm, cells, sems.at[2, 1]),
        pltpu.make_async_copy(misfit_hbm, misfit, sems.at[2, 2]),
    ]
    for side, start in ((0, 0), (1, ROWS - 8)):
        for tile in range(TILES):
            at = pl.ds(tile * 128, 128)
            copies.append(
                pltpu.make_async_copy(adjoint.at[:, pl.ds(start, 8), at], rows_buf.at[side, tile], sems.at[side, tile])
            )
        copies.append(pltpu.make_async_copy(velocity.at[1, :, pl.ds(start, 8), :], u_buf.at[side], sems.at[side, TILES]))
        copies.append(pltpu.make_async_copy(density.at[1, pl.ds(start, 8), :], rho_buf.at[side], sems.at[side, TILES + 1]))
    for copy in copies:
        copy.start()
    for copy in copies:
        copy.wait()
    flat = rows_buf.reshape(2, TILES, K * 8, 128)

    def pack(side, out):
        slot = 0 if side == "lo" else 1
        first = 0 if side == "lo" else 7
        second = 1 if side == "lo" else 6
        for tile in range(TILES):
            at = pl.ds(tile * 128, 128)
            out[0:8, at] = flat[slot, tile, pl.ds(first, 8, stride=8), :]
            out[8:16, at] = flat[slot, tile, pl.ds(64 + first, 8, stride=8), :]
            out[16:19, at] = flat[slot, tile, pl.ds(128 + first, 3, stride=8), :]
            for index, number in enumerate(X_SIDE[side]):
                out[19 + index : 20 + index, at] = rows_buf[slot, tile, number, second : second + 1, :]
        for axis in range(3):
            out[24 + axis : 25 + axis, :] = u_buf[slot, axis, first : first + 1, :]
        out[27:28, :] = rho_buf[slot, first : first + 1, :]
        edge = 0 if side == "lo" else ROWS - 1
        inner = 1 if side == "lo" else ROWS - 2
        out[28:29, 0:COLS] = heights[edge : edge + 1, :].astype(F32)
        out[28:29, 128 : 128 + COLS] = heights[inner : inner + 1, :].astype(F32)
        out[28:29, 256:384] = cells[0].astype(F32)
        for axis in range(3):
            out[28:29, 384 + 128 * axis : 512 + 128 * axis] = misfit[1, axis, 0]

    def even():
        pack("hi", out_a)
        pack("lo", out_b)

    def odd():
        pack("lo", out_a)
        pack("hi", out_b)

    by_parity(lax.axis_index("gx") % 2, even, odd)


def pack_x(adjoint, velocity, density, heights, cells, misfit):
    shape = jax.ShapeDtypeStruct((X_FIELDS, TILES * 128), F32)
    return pl.pallas_call(
        pack_x_kernel,
        out_shape=(shape, shape),
        in_specs=[HBM] * 6,
        out_specs=(VMEM, VMEM),
        scratch_shapes=[
            pltpu.VMEM((2, TILES, K, 8, 128), F32),
            pltpu.VMEM((2, 3, 8, TILES * 128), F32),
            pltpu.VMEM((2, 8, TILES * 128), F32),
            pltpu.VMEM((ROWS, COLS), jnp.int32),
            pltpu.VMEM((1, 1, SENS), jnp.int32),
            pltpu.VMEM((2, 3, 1, 1, SENS), F32),
            pltpu.SemaphoreType.DMA((3, TILES + 2)),
        ],
        compiler_params=pltpu.CompilerParams(vmem_limit_bytes=8 * MB),
        name="pack_x",
    )(adjoint, velocity, density, heights, cells, misfit)


def place_x(message, side, slot, tile, field, u):
    outer, inner = (BASE + ROWS, BASE + ROWS + 1) if side == "lo" else (BASE - 1, BASE - 2)
    flat = field.reshape(field.shape[0], K * EXT, 128)
    at = pl.ds(tile * 128, 128)
    flat[slot, pl.ds(outer, 8, stride=EXT), :] = message[0:8, at]
    flat[slot, pl.ds(8 * EXT + outer, 8, stride=EXT), :] = message[8:16, at]
    flat[slot, pl.ds(16 * EXT + outer, 3, stride=EXT), :] = message[16:19, at]
    for index, number in enumerate(X_SIDE[side]):
        field[slot, number, inner : inner + 1, :] = message[19 + index : 20 + index, at]
    for axis in range(3):
        u[slot, 1, axis, outer : outer + 1, :] = message[24 + axis : 25 + axis, at]


def place_tall(message, side, tall):
    outer, inner = (BASE + ROWS, BASE + ROWS + 1) if side == "lo" else (BASE - 1, BASE - 2)
    tall[outer : outer + 1, 0:COLS] = message[28:29, 0:COLS]
    tall[inner : inner + 1, 0:COLS] = message[28:29, 128 : 128 + COLS]


def edge_sensors(message, side):
    numbers = message[28:29, 256:384].astype(jnp.int32)
    here = numbers // (COLS * NZ) == (0 if side == "lo" else ROWS - 1)
    rows = [
        jnp.where(here, message[28:29, 384 + 128 * axis : 512 + 128 * axis], 0.0) for axis in range(3)
    ]
    parts = split3(jnp.concatenate(rows + [jnp.zeros((5, SENS), F32)], axis=0))
    return jnp.concatenate(parts + (jnp.zeros((8, SENS), jnp.bfloat16),), axis=0), numbers % (COLS * NZ)


def one_hot(lane, tile, width):
    cells = lax.broadcasted_iota(jnp.int32, (width, SENS), 0) + tile * 128
    return jnp.where(cells == lane, 1.0, 0.0).astype(jnp.bfloat16)


def product(left, right):
    return lax.dot_general(left, right, (((1,), (1,)), ((), ())), preferred_element_type=F32)


def place_force(message, side, sensors, slot, tile, force):
    outer = BASE + ROWS if side == "lo" else BASE - 1
    left, lane = sensors
    parts = product(left, one_hot(lane, tile, 128))
    total = parts[0:8] + (parts[8:16] + parts[16:24])
    scaled = total * (1.0 / message[27:28, pl.ds(tile * 128, 128)])
    for axis in range(3):
        force[slot, 1, axis, outer : outer + 1, :] = scaled[axis : axis + 1]


def column_tops(tall, tile, rows):
    at = slice(rows, rows + 8)
    low = lanes() < NZ
    left = jnp.broadcast_to(tall[at, 2 * tile : 2 * tile + 1], (8, 128))
    right = jnp.broadcast_to(tall[at, 2 * tile + 1 : 2 * tile + 2], (8, 128))
    return jnp.where(low, left, right)


def shifted_tops(geo, tops, tile, rows):
    at = pl.ds(rows, 8)
    after, before = (tile + 1) % (TILES + 1), (tile - 1) % (TILES + 1)
    here = tops[0, tile, at, :]
    tops[1, tile, at, :] = half_turn(from_next(geo, here, tops[0, after, at, :]))
    tops[2, tile, at, :] = half_turn(from_previous(geo, here, tops[0, before, at, :]))


def step(geo, number_of_step, source, target, u, force, tops, starts, tile, after, before):
    def read(where, number, row):
        return source[where, number, pl.ds(row, 8), :]

    def top(cy, row):
        return tops[cy % 3, tile, pl.ds(row, 8), :]

    for start in starts:
        at = pl.ds(start, 8)
        f = incoming(geo, read, top, tile, after, before, start, range(K))
        velocity = [u[tile, number_of_step, axis, at, :] for axis in range(3)]
        push = [force[tile, number_of_step, axis, at, :] for axis in range(3)]
        fluid = geo.level >= tops[0, tile, at, :]
        result = collide(f, velocity, push, range(K), fluid)
        for number in range(K):
            target[tile, number, at, :] = result[number]


WIDE = TILES + 1
FIELD = jax.ShapeDtypeStruct((WIDE, K, EXT, 128), F32)
VECTORS = jax.ShapeDtypeStruct((TILES, 2, 3, EXT, 128), F32)
TOPS = jax.ShapeDtypeStruct((3, WIDE, EXT, 128), F32)
TALL = jax.ShapeDtypeStruct((EXT, 128), F32)


def prepare_kernel(adjoint, velocity, density, heights_hbm, cells_hbm, misfit_hbm,
                   field, middle, u, force, tops, tall, rho, heights, cells, misfit, sems):
    own = pl.ds(BASE, ROWS)
    small = [
        pltpu.make_async_copy(heights_hbm, heights, sems.at[2, 1]),
        pltpu.make_async_copy(cells_hbm, cells, sems.at[2, 2]),
        pltpu.make_async_copy(misfit_hbm, misfit, sems.at[2, 3]),
    ]
    for copy in small:
        copy.start()
    loads = [pltpu.make_async_copy(density, rho, sems.at[2, 0])]
    for tile in range(TILES):
        at = pl.ds(tile * 128, 128)
        loads.append(pltpu.make_async_copy(adjoint.at[:, :, at], field.at[tile, :, own, :], sems.at[0, tile]))
    for tile in range(TILES):
        at = pl.ds(tile * 128, 128)
        loads.append(pltpu.make_async_copy(velocity.at[:, :, :, at], u.at[tile, :, :, own, :], sems.at[1, tile]))
    for copy in loads:
        copy.start()
    geo = Geometry()
    for copy in small:
        copy.wait()
    tall[BASE : BASE + ROWS, 0:COLS] = heights[...].astype(F32)
    for tile in range(TILES):
        for row in range(BASE, BASE + ROWS, 8):
            tops[0, tile, row : row + 8] = column_tops(tall, tile, row)
    for tile in range(1, TILES - 1):
        for row in range(BASE, BASE + ROWS, 8):
            shifted_tops(geo, tops, tile, row)

    numbers = cells[0]
    row = numbers // (COLS * NZ)
    lane = numbers % (COLS * NZ)
    here = lax.broadcasted_iota(jnp.int32, (ROWS, SENS), 0) == row
    parts = []
    for back in range(2):
        for axis in range(3):
            parts.append(split3(jnp.where(here, misfit[back, axis, 0], 0.0)))
    left = jnp.concatenate(
        [jnp.concatenate([part[index] for part in parts], axis=0) for index in range(3)], axis=1
    )
    loads[0].wait()
    for pair in range(TILES // 2):
        right = one_hot(lane, 2 * pair, 256)
        summed = product(left, jnp.concatenate([right, right, right], axis=1))
        for half in range(2):
            tile = 2 * pair + half
            at = pl.ds(tile * 128, 128)
            for back in range(2):
                inverse = 1.0 / rho[back, :, at]
                for axis in range(3):
                    first = (3 * back + axis) * ROWS
                    force[tile, back, axis, own, :] = (
                        summed[first : first + ROWS, 128 * half : 128 * half + 128] * inverse
                    )
    for copy in loads[1:]:
        copy.wait()

    def inner(tile, carry):
        step(geo, 1, field, middle, u, force, tops, STARTS_INNER, tile, tile + 1, tile - 1)
        return carry

    lax.fori_loop(1, TILES - 1, inner, 0)


def prepare(adjoint, velocity, density, heights, cells, misfit):
    return pl.pallas_call(
        prepare_kernel,
        out_shape=(FIELD, FIELD, VECTORS, VECTORS, TOPS, TALL),
        in_specs=[HBM] * 6,
        out_specs=(VMEM,) * 6,
        scratch_shapes=[
            pltpu.VMEM((2, ROWS, TILES * 128), F32),
            pltpu.VMEM((ROWS, COLS), jnp.int32),
            pltpu.VMEM((1, 1, SENS), jnp.int32),
            pltpu.VMEM((2, 3, 1, 1, SENS), F32),
            pltpu.SemaphoreType.DMA((3, TILES)),
        ],
        compiler_params=pltpu.CompilerParams(vmem_limit_bytes=PREPARE_VMEM),
        cost_estimate=pl.CostEstimate(flops=40_000_000, bytes_accessed=8_000_000, transcendentals=0),
        name="prepare",
    )(adjoint, velocity, density, heights, cells, misfit)


def pack_y_kernel(own_tall, all_field, all_u, all_force, msg_a, msg_b,
                  out_a, out_b, field, u, force, tall, tops, partial):
    slots = ((0, 0), (1, TILES - 1))
    own = pl.ds(BASE, ROWS)
    for slot, tile in slots:
        field[slot, :, own, :] = all_field[tile, :, own, :]
        u[slot, 1, :, own, :] = all_u[tile, 1, :, own, :]
        force[slot, 1, :, own, :] = all_force[tile, 1, :, own, :]
    tall[BASE : BASE + ROWS] = own_tall[BASE : BASE + ROWS]
    geo = Geometry()

    def from_x(low_msg, high_msg):
        for message, side in ((low_msg, "lo"), (high_msg, "hi")):
            place_tall(message, side, tall)
            sensors = edge_sensors(message, side)
            for slot, tile in slots:
                place_x(message, side, slot, tile, field, u)
                place_force(message, side, sensors, slot, tile, force)

    by_parity(lax.axis_index("gx") % 2, lambda: from_x(msg_a, msg_b), lambda: from_x(msg_b, msg_a))
    for slot, tile in slots:
        for row in range(0, EXT, 8):
            value = column_tops(tall, tile, row)
            tops[slot, 0, row : row + 8] = value
            tops[slot, 1, row : row + 8] = half_turn(value)

    def read(tile, number, row):
        return field[tile, number, pl.ds(row, 8), :]

    for slot, side in ((0, "lo"), (1, "hi")):
        inward = 1 if side == "lo" else -1
        numbers = [n for n in range(K) if VELOCITIES[n][1] in (0, inward)]
        for start in STARTS_WIDE:
            at = pl.ds(start, 8)

            def top(cy, row, slot=slot):
                return tops[slot, 0 if cy == 0 else 1, pl.ds(row, 8), :]

            f = incoming(geo, read, top, slot, slot, slot, start, numbers)
            velocity_here = [u[slot, 1, axis, at, :] for axis in range(3)]
            push = [force[slot, 1, axis, at, :] for axis in range(3)]
            fluid = geo.level >= tops[slot, 0, at, :]
            result = collide(f, velocity_here, push, Y_SIDE[side], fluid)
            for index, number in enumerate(Y_SIDE[side]):
                partial[slot, index, at, :] = result[number]

    def write(side, out):
        slot = 0 if side == "lo" else 1
        for start in range(0, 40, 8):
            at = pl.ds(start + BASE - 2, 8)
            pairs = [
                (field[slot, number, at, :], partial[slot, index, at, :])
                for index, number in enumerate(Y_SIDE[side])
            ]
            pairs.append((u[slot, 1, 0, at, :], u[slot, 1, 1, at, :]))
            pairs.append((u[slot, 1, 2, at, :], tops[slot, 0, at, :]))
            for index, (first, second) in enumerate(pairs):
                turned = half_turn(second)
                if side == "lo":
                    value = jnp.where(geo.low, first, turned)
                else:
                    value = jnp.where(geo.low, turned, first)
                out[index, start : start + 8, :] = value

    def even():
        write("hi", out_a)
        write("lo", out_b)

    def odd():
        write("lo", out_a)
        write("hi", out_b)

    by_parity(lax.axis_index("gy") % 2, even, odd)


def pack_y(heights, field, u, force, msg_a, msg_b):
    shape = jax.ShapeDtypeStruct((Y_FIELDS, 40, 128), F32)
    return pl.pallas_call(
        pack_y_kernel,
        out_shape=(shape, shape),
        in_specs=[VMEM] * 6,
        out_specs=(VMEM, VMEM),
        scratch_shapes=[
            pltpu.VMEM((2, K, EXT, 128), F32),
            pltpu.VMEM((2, 2, 3, EXT, 128), F32),
            pltpu.VMEM((2, 2, 3, EXT, 128), F32),
            pltpu.VMEM((EXT, 128), F32),
            pltpu.VMEM((2, 2, EXT, 128), F32),
            pltpu.VMEM((2, 5, EXT, 128), F32),
        ],
        compiler_params=pltpu.CompilerParams(vmem_limit_bytes=SMALL_VMEM),
        name="pack_y",
    )(heights, field, u, force, msg_a, msg_b)


def send_out(field, out, sems, tile):
    at = pl.ds(pl.multiple_of(tile * 128, 128), 128)
    return pltpu.make_async_copy(field.at[tile, :, pl.ds(BASE, ROWS), :], out.at[:, :, at], sems.at[tile])


def inner_kernel(own_tall, msg_a, msg_b, order, field_in, middle_in, u_in, force_in, tops_in,
                 field, middle, u, force, tops, out, tall, sems):
    del order, field_in, middle_in, u_in, force_in, tops_in
    geo = Geometry()
    tall[BASE : BASE + ROWS] = own_tall[BASE : BASE + ROWS]

    def from_x(low_msg, high_msg):
        for message, side in ((low_msg, "lo"), (high_msg, "hi")):
            place_tall(message, side, tall)
            sensors = edge_sensors(message, side)
            for tile in range(TILES):
                place_x(message, side, tile, tile, field, u)
                place_force(message, side, sensors, tile, tile, force)

    by_parity(lax.axis_index("gx") % 2, lambda: from_x(msg_a, msg_b), lambda: from_x(msg_b, msg_a))
    for tile in range(TILES):
        for row in (0, BASE + ROWS):
            tops[0, tile, row : row + 8] = column_tops(tall, tile, row)
    for tile in range(1, TILES - 1):
        for row in (0, BASE + ROWS):
            shifted_tops(geo, tops, tile, row)

    def edges(tile, carry):
        step(geo, 1, field, middle, u, force, tops, STARTS_EDGE, tile, tile + 1, tile - 1)
        return carry

    lax.fori_loop(1, TILES - 1, edges, 0)

    def second(tile, carry):
        step(geo, 0, middle, field, u, force, tops, STARTS_OWN, tile, tile + 1, tile - 1)
        send_out(field, out, sems, tile).start()
        return carry

    def sent(tile, carry):
        send_out(field, out, sems, tile).wait()
        return carry

    lax.fori_loop(2, TILES - 2, second, 0)
    lax.fori_loop(2, TILES - 2, sent, 0)


def inner_columns(heights, msg_a, msg_b, order, field, middle, u, force, tops, shape):
    return pl.pallas_call(
        inner_kernel,
        out_shape=(FIELD, FIELD, VECTORS, VECTORS, TOPS, jax.ShapeDtypeStruct(shape, F32)),
        in_specs=[VMEM] * 3 + [HBM] + [VMEM] * 5,
        out_specs=(VMEM,) * 5 + (HBM,),
        input_output_aliases={4: 0, 5: 1, 6: 2, 7: 3, 8: 4},
        scratch_shapes=[pltpu.VMEM((EXT, 128), F32), pltpu.SemaphoreType.DMA((TILES,))],
        compiler_params=pltpu.CompilerParams(vmem_limit_bytes=SMALL_VMEM),
        cost_estimate=pl.CostEstimate(flops=40_000_000, bytes_accessed=8_000_000, transcendentals=0),
        name="inner_columns",
    )(heights, msg_a, msg_b, order, field, middle, u, force, tops)


def outer_kernel(msg_a, msg_b, field_in, middle_in, u, force, tops_in, out_in,
                 field, middle, tops, out, side_partial, side_u, sems):
    del field_in, middle_in, tops_in, out_in
    geo = Geometry()

    def from_y(low_msg, high_msg):
        for start in range(0, 40, 8):
            at = pl.ds(start + BASE - 2, 8)
            for index in range(Y_FIELDS):
                low_value = low_msg[index, start : start + 8, :]
                high_value = high_msg[index, start : start + 8, :]
                low_turned, high_turned = half_turn(low_value), half_turn(high_value)
                if index < 5:
                    field[TILES, Y_SIDE["lo"][index], at, :] = low_value
                    field[TILES, Y_SIDE["hi"][index], at, :] = high_value
                    side_partial[0, index, at, :] = low_turned
                    side_partial[1, index, at, :] = high_turned
                else:
                    first = jnp.where(geo.low, low_value, high_value)
                    second = jnp.where(geo.low, low_turned, high_turned)
                    if index == 5:
                        side_u[0, at, :] = first
                        side_u[1, at, :] = second
                    else:
                        side_u[2, at, :] = first
                        tops[0, TILES, at, :] = second

    by_parity(lax.axis_index("gy") % 2, lambda: from_y(msg_a, msg_b), lambda: from_y(msg_b, msg_a))
    for tile in (0, TILES - 1, TILES):
        for row in range(0, EXT, 8):
            shifted_tops(geo, tops, tile, row)
    for tile, after, before in ((0, 1, TILES), (TILES - 1, TILES, TILES - 2)):
        step(geo, 1, field, middle, u, force, tops, STARTS_WIDE, tile, after, before)

    def read(where, number, row):
        return field[where, number, pl.ds(row, 8), :]

    def top(cy, row):
        return tops[cy % 3, TILES, pl.ds(row, 8), :]

    for slot, side, other in ((0, "lo", "hi"), (1, "hi", "lo")):
        for start in STARTS_WIDE:
            at = pl.ds(start, 8)
            f = incoming(geo, read, top, TILES, 0, TILES - 1, start, Y_SIDE[other])
            velocity = [side_u[axis, at, :] for axis in range(3)]
            fluid = geo.level >= tops[0, TILES, at, :]
            result = collide(f, velocity, None, Y_SIDE[side], fluid)
            for index, number in enumerate(Y_SIDE[side]):
                middle[TILES, number, at, :] = result[number] + side_partial[slot, index, at, :]

    last = (1, TILES - 2, 0, TILES - 1)
    for tile in last:
        before = TILES if tile == 0 else tile - 1
        step(geo, 0, middle, field, u, force, tops, STARTS_OWN, tile, tile + 1, before)
        send_out(field, out, sems, tile).start()
    for tile in last:
        send_out(field, out, sems, tile).wait()


def outer_columns(msg_a, msg_b, field, middle, u, force, tops, out):
    return pl.pallas_call(
        outer_kernel,
        out_shape=(FIELD, FIELD, TOPS, jax.ShapeDtypeStruct(out.shape, F32)),
        in_specs=[VMEM] * 7 + [HBM],
        out_specs=(VMEM,) * 3 + (HBM,),
        input_output_aliases={2: 0, 3: 1, 6: 2, 7: 3},
        scratch_shapes=[
            pltpu.VMEM((2, 5, EXT, 128), F32),
            pltpu.VMEM((3, EXT, 128), F32),
            pltpu.SemaphoreType.DMA((TILES,)),
        ],
        compiler_params=pltpu.CompilerParams(vmem_limit_bytes=SMALL_VMEM),
        name="outer_columns",
    )(msg_a, msg_b, field, middle, u, force, tops, out)


def partners(count, odd):
    if not odd:
        return [(i, i ^ 1) for i in range(count)]
    return [(i, (i - 1) % count if i % 2 == 0 else (i + 1) % count) for i in range(count)]


def swap(value, axis, odd):
    return lax.ppermute(value, axis, partners(lax.axis_size(axis), odd))


def per_device(adjoint, velocity, density, heights, cells, misfit):
    args = [
        pltpu.with_memory_space_constraint(value, pltpu.HBM)
        for value in (adjoint, velocity, density, heights, cells, misfit)
    ]
    x_a, x_b = pack_x(*args)
    x_a, x_b = swap(x_a, "gx", False), swap(x_b, "gx", True)
    field, middle, u, force, tops, tall = prepare(*args)
    own_a, own_b = pack_y(tall, field, u, force, x_a, x_b)
    y_a, y_b = swap(own_a, "gy", False), swap(own_b, "gy", True)
    field, middle, u, force, tops, out = inner_columns(
        tall, x_a, x_b, own_a, field, middle, u, force, tops, adjoint.shape
    )
    return outer_columns(y_a, y_b, field, middle, u, force, tops, out)[3]


def solution(mesh):
    return jax.shard_map(
        per_device,
        mesh=mesh,
        in_specs=(
            P(None, "gx", "gy"),
            P(None, None, "gx", "gy"),
            P(None, "gx", "gy"),
            P("gx", "gy"),
            P("gx", "gy", None),
            P(None, None, "gx", "gy", None),
        ),
        out_specs=P(None, "gx", "gy"),
        check_vma=False,
    )
```

```python
import functools

import jax
import jax.numpy as jnp
from jax import lax
from jax.experimental import pallas as pl
from jax.experimental.pallas import tpu as pltpu
from jax.sharding import PartitionSpec as P

VELOCITIES = (
    (0, 0, 0),
    (1, 0, 0),
    (-1, 0, 0),
    (0, 1, 0),
    (0, -1, 0),
    (0, 0, 1),
    (0, 0, -1),
    (1, 1, 0),
    (-1, -1, 0),
    (1, -1, 0),
    (-1, 1, 0),
    (1, 0, 1),
    (-1, 0, -1),
    (1, 0, -1),
    (-1, 0, 1),
    (0, 1, 1),
    (0, -1, -1),
    (0, 1, -1),
    (0, -1, 1),
)
OPPOSITE = (0, 2, 1, 4, 3, 6, 5, 8, 7, 10, 9, 12, 11, 14, 13, 16, 15, 18, 17)
K = 19
ROWS, COLS, NZ = 32, 32, 64
TILES = COLS * NZ // 128
EXT = 48
BASE = 8
SENS = 128
STARTS_WIDE = (7, 15, 23, 31, 33)
STARTS_OWN = (8, 16, 24, 32)
STARTS_INNER = (9, 17, 25, 31)
STARTS_EDGE = (7, 33)
X_SIDE = {"lo": (1, 7, 9, 11, 13), "hi": (2, 8, 10, 12, 14)}
Y_SIDE = {"lo": (3, 7, 10, 15, 17), "hi": (4, 8, 9, 16, 18)}
X_FIELDS = 32
Y_FIELDS = 7
F32 = jnp.float32
MB = 1024 * 1024
PREPARE_VMEM = 4 * MB
SMALL_VMEM = 4 * MB
HBM = pl.BlockSpec(memory_space=pltpu.HBM)
VMEM = pl.BlockSpec(memory_space=pltpu.VMEM)


def add(a, b):
    if a is None:
        return b
    return a if b is None else a + b


def sub(a, b):
    if b is None:
        return a
    return -b if a is None else a - b


def lanes():
    return lax.broadcasted_iota(jnp.int32, (8, 128), 1)


class Geometry:
    def __init__(self):
        lane = lanes()
        level = lane % NZ
        self.low = lane < NZ
        self.level = level.astype(F32)
        up = jnp.where(level == NZ - 1, -1, level + 1).astype(F32)
        self.raised = {0: self.level, 1: up, -1: self.level - 1.0}


def half_turn(value):
    return pltpu.roll(value, NZ, 1)


def from_next(geo, here, after):
    return jnp.where(geo.low, after, here)


def from_previous(geo, here, before):
    return jnp.where(geo.low, here, before)


def pull(geo, read, tile, after, before, position, number):
    cx, cy, cz = VELOCITIES[number]
    row = position + cx
    if cy == 0:
        value = read(tile, number, row)
        return pltpu.roll(value, (128 - cz) % 128, 1) if cz else value
    if cy == 1:
        value = from_next(geo, read(tile, number, row), read(after, number, row))
    else:
        value = from_previous(geo, read(tile, number, row), read(before, number, row))
    return pltpu.roll(value, NZ - cz, 1)


def incoming(geo, read, tops, tile, after, before, position, numbers):
    out = [None] * K
    for number in numbers:
        cx, cy, cz = VELOCITIES[number]
        value = pull(geo, read, tile, after, before, position, number)
        if number:
            blocked = geo.raised[cz] < tops(cy, position + cx)
            value = jnp.where(blocked, read(tile, OPPOSITE[number], position), value)
        out[number] = value
    return out


def moments(f):
    plus = [None] * K
    minus = [None] * K
    for number in range(1, K, 2):
        plus[number] = add(f[number], f[number + 1])
        minus[number] = sub(f[number], f[number + 1])
    sxy, dxy = add(plus[7], plus[9]), sub(plus[7], plus[9])
    sxz, dxz = add(plus[11], plus[13]), sub(plus[11], plus[13])
    syz, dyz = add(plus[15], plus[17]), sub(plus[15], plus[17])
    twice = [None if plus[n] is None else plus[n] + plus[n] for n in (1, 3, 5)]
    mxx = add(twice[0], add(sxy, sxz))
    myy = add(twice[1], add(sxy, syz))
    mzz = add(twice[2], add(sxz, syz))
    total = add(add(add(twice[0], twice[1]), twice[2]), add(add(sxy, sxz), syz))
    if f[0] is not None:
        total = add(12.0 * f[0], total)

    def axis(main, first, second):
        doubled = None if minus[main] is None else minus[main] + minus[main]
        return add(doubled, add(first, second))

    jx = axis(1, add(minus[7], minus[9]), add(minus[11], minus[13]))
    jy = axis(3, sub(minus[7], minus[9]), add(minus[15], minus[17]))
    jz = axis(5, sub(minus[11], minus[13]), sub(minus[15], minus[17]))
    return total, (jx, jy, jz), (mxx, myy, mzz, dxy, dxz, dyz)


def mul(a, b):
    return None if a is None else a * b


SCALES = {1: (1.0, -1.25), 0: (-0.8, 1.0)}


def collide(f, u, force, numbers, number_of_step):
    read_scale, write_scale = SCALES[number_of_step]
    scale = read_scale * write_scale
    total, (jx, jy, jz), (mxx, myy, mzz, dxy, dxz, dyz) = moments(f)
    ux, uy, uz = u
    sx, sy, sz = (0.225 * scale) * ux, (0.225 * scale) * uy, (0.225 * scale) * uz
    qx = add(add(mul(mxx, sx), mul(dxy, sy)), mul(dxz, sz))
    qy = add(add(mul(dxy, sx), mul(myy, sy)), mul(dyz, sz))
    qz = add(add(mul(dxz, sx), mul(dyz, sy)), mul(mzz, sz))
    q = (qx, qy, qz)
    pushed = q if force is None else [q[axis] + force[axis] for axis in range(3)]
    speed = ux * ux + uy * uy + uz * uz
    scalar = total * (0.05 * scale + (0.075 * scale) * speed)
    scalar = scalar - (ux * pushed[0] + uy * pushed[1] + uz * pushed[2])
    scaled = (0.15 * scale) * total
    vector = []
    for axis, j in enumerate((jx, jy, jz)):
        value = q[axis] + pushed[axis] - scaled * u[axis]
        vector.append(add(mul(j, 0.15 * scale), value))
    out = {}
    along = {}
    for number in numbers:
        pair = number if number % 2 else number - 1
        if number == 0:
            value = scalar
        else:
            if pair not in along:
                first = VELOCITIES[pair]
                cv = None
                for axis in range(3):
                    if first[axis] == 1:
                        cv = add(cv, vector[axis])
                    elif first[axis] == -1:
                        cv = sub(cv, vector[axis])
                along[pair] = cv
            value = scalar + along[pair] if number == pair else scalar - along[pair]
        if f[number] is not None:
            value = value + (f[number] if number_of_step == 1 else (-0.8 * scale) * f[number])
        out[number] = value
    return out


def split(value):
    high = value.astype(jnp.bfloat16)
    return high, (value - high.astype(F32)).astype(jnp.bfloat16)


def one_hot(lane, tile, width):
    cells = lax.broadcasted_iota(jnp.int32, (width, SENS), 0) + tile * 128
    return jnp.where(cells == lane, 1.0, 0.0).astype(jnp.bfloat16)


def product(left, right):
    return lax.dot_general(left, right, (((1,), (1,)), ((), ())), preferred_element_type=F32)


def by_parity(parity, upper, lower):
    pl.when(parity == 1)(upper)
    pl.when(parity == 0)(lower)


def pack_x_kernel(adjoint, velocity, density, heights_hbm, cells_hbm, misfit_hbm, out_a, out_b,
                  rows_buf, u_buf, rho_buf, heights, cells, misfit, edge_force, sems):
    copies = [
        pltpu.make_async_copy(heights_hbm, heights, sems.at[2, 0]),
        pltpu.make_async_copy(cells_hbm, cells, sems.at[2, 1]),
        pltpu.make_async_copy(misfit_hbm, misfit, sems.at[2, 2]),
    ]
    for side, start in ((0, 0), (1, ROWS - 8)):
        for tile in range(TILES):
            at = pl.ds(tile * 128, 128)
            copies.append(
                pltpu.make_async_copy(adjoint.at[:, pl.ds(start, 8), at], rows_buf.at[side, tile], sems.at[side, tile])
            )
        copies.append(pltpu.make_async_copy(velocity.at[1, :, pl.ds(start, 8), :], u_buf.at[side], sems.at[side, TILES]))
        copies.append(pltpu.make_async_copy(density.at[1, pl.ds(start, 8), :], rho_buf.at[side], sems.at[side, TILES + 1]))
    for copy in copies:
        copy.start()
    for copy in copies[:3]:
        copy.wait()
    numbers = cells[0]
    lane = numbers % (COLS * NZ)
    parts = []
    for edge in (0, ROWS - 1):
        here = numbers // (COLS * NZ) == edge
        rows = [jnp.where(here, SCALES[1][1] * misfit[1, axis, 0], 0.0) for axis in range(3)]
        parts.append(split(jnp.concatenate(rows + [jnp.zeros((5, SENS), F32)], axis=0)))
    left = jnp.concatenate(
        [jnp.concatenate([part[index] for part in parts], axis=0) for index in range(2)], axis=1
    )
    for pair in range(TILES // 2):
        right = one_hot(lane, 2 * pair, 256)
        edge_force[:, pl.ds(256 * pair, 256)] = product(left, jnp.concatenate([right, right], axis=1))
    for copy in copies[3:]:
        copy.wait()
    flat = rows_buf.reshape(2, TILES, K * 8, 128)

    def pack(side, out):
        slot = 0 if side == "lo" else 1
        first = 0 if side == "lo" else 7
        second = 1 if side == "lo" else 6
        for tile in range(TILES):
            at = pl.ds(tile * 128, 128)
            out[0:8, at] = flat[slot, tile, pl.ds(first, 8, stride=8), :]
            out[8:16, at] = flat[slot, tile, pl.ds(64 + first, 8, stride=8), :]
            out[16:19, at] = flat[slot, tile, pl.ds(128 + first, 3, stride=8), :]
            for index, number in enumerate(X_SIDE[side]):
                out[19 + index : 20 + index, at] = rows_buf[slot, tile, number, second : second + 1, :]
        inverse = 1.0 / rho_buf[slot, first : first + 1, :]
        out[24:27, :] = edge_force[8 * slot : 8 * slot + 3, :] * inverse
        for axis in range(3):
            out[27 + axis : 28 + axis, :] = u_buf[slot, axis, first : first + 1, :]
        edge = 0 if side == "lo" else ROWS - 1
        inner = 1 if side == "lo" else ROWS - 2
        out[30:31, 0:COLS] = heights[edge : edge + 1, :].astype(F32)
        out[30:31, 128 : 128 + COLS] = heights[inner : inner + 1, :].astype(F32)

    def upper():
        pack("hi", out_a)
        pack("lo", out_b)

    def lower():
        pack("lo", out_a)
        pack("hi", out_b)

    by_parity(lax.axis_index("gx") % 2, upper, lower)


def pack_x(adjoint, velocity, density, heights, cells, misfit):
    shape = jax.ShapeDtypeStruct((X_FIELDS, TILES * 128), F32)
    return pl.pallas_call(
        pack_x_kernel,
        out_shape=(shape, shape),
        in_specs=[HBM] * 6,
        out_specs=(VMEM, VMEM),
        scratch_shapes=[
            pltpu.VMEM((2, TILES, K, 8, 128), F32),
            pltpu.VMEM((2, 3, 8, TILES * 128), F32),
            pltpu.VMEM((2, 8, TILES * 128), F32),
            pltpu.VMEM((ROWS, COLS), jnp.int32),
            pltpu.VMEM((1, 1, SENS), jnp.int32),
            pltpu.VMEM((2, 3, 1, 1, SENS), F32),
            pltpu.VMEM((16, TILES * 128), F32),
            pltpu.SemaphoreType.DMA((3, TILES + 2)),
        ],
        compiler_params=pltpu.CompilerParams(vmem_limit_bytes=8 * MB),
        name="pack_x",
    )(adjoint, velocity, density, heights, cells, misfit)


def place_x(message, side, slot, tile, field, u, force):
    outer, inner = (BASE + ROWS, BASE + ROWS + 1) if side == "lo" else (BASE - 1, BASE - 2)
    flat = field.reshape(field.shape[0], K * EXT, 128)
    at = pl.ds(tile * 128, 128)
    flat[slot, pl.ds(outer, 8, stride=EXT), :] = message[0:8, at]
    flat[slot, pl.ds(8 * EXT + outer, 8, stride=EXT), :] = message[8:16, at]
    flat[slot, pl.ds(16 * EXT + outer, 3, stride=EXT), :] = message[16:19, at]
    for index, number in enumerate(X_SIDE[side]):
        field[slot, number, inner : inner + 1, :] = message[19 + index : 20 + index, at]
    for axis in range(3):
        force[slot, 1, axis, outer : outer + 1, :] = message[24 + axis : 25 + axis, at]
        u[slot, 1, axis, outer : outer + 1, :] = message[27 + axis : 28 + axis, at]


def place_tall(message, side, tall):
    outer, inner = (BASE + ROWS, BASE + ROWS + 1) if side == "lo" else (BASE - 1, BASE - 2)
    tall[outer : outer + 1, 0:COLS] = message[30:31, 0:COLS]
    tall[inner : inner + 1, 0:COLS] = message[30:31, 128 : 128 + COLS]


def column_tops(tall, tile, rows):
    at = slice(rows, rows + 8)
    low = lanes() < NZ
    left = jnp.broadcast_to(tall[at, 2 * tile : 2 * tile + 1], (8, 128))
    right = jnp.broadcast_to(tall[at, 2 * tile + 1 : 2 * tile + 2], (8, 128))
    return jnp.where(low, left, right)


def shifted_tops(geo, tops, tile, rows):
    at = pl.ds(rows, 8)
    after, before = (tile + 1) % (TILES + 1), (tile - 1) % (TILES + 1)
    here = tops[0, tile, at, :]
    tops[1, tile, at, :] = half_turn(from_next(geo, here, tops[0, after, at, :]))
    tops[2, tile, at, :] = half_turn(from_previous(geo, here, tops[0, before, at, :]))


def step(geo, number_of_step, source, target, u, force, tops, starts, tile, after, before):
    def read(where, number, row):
        return source[where, number, pl.ds(row, 8), :]

    def top(cy, row):
        return tops[cy % 3, tile, pl.ds(row, 8), :]

    for start in starts:
        at = pl.ds(start, 8)
        f = incoming(geo, read, top, tile, after, before, start, range(K))
        velocity = [u[tile, number_of_step, axis, at, :] for axis in range(3)]
        push = [force[tile, number_of_step, axis, at, :] for axis in range(3)]
        result = collide(f, velocity, push, range(K), number_of_step)
        if number_of_step:
            for number in range(K):
                target[tile, number, at, :] = result[number]
        else:
            fluid = geo.level >= tops[0, tile, at, :]
            for number in range(K):
                target[tile, number, at, :] = jnp.zeros((8, 128), F32)
                pltpu.store(target.at[tile, number, at, :], result[number], mask=fluid)


WIDE = TILES + 1
FIELD = jax.ShapeDtypeStruct((WIDE, K, EXT, 128), F32)
VECTORS = jax.ShapeDtypeStruct((TILES, 2, 3, EXT, 128), F32)
TOPS = jax.ShapeDtypeStruct((3, WIDE, EXT, 128), F32)
TALL = jax.ShapeDtypeStruct((EXT, 128), F32)


def prepare_kernel(adjoint, velocity, density, heights_hbm, cells_hbm, misfit_hbm,
                   field, middle, u, force, tops, tall, rho, heights, cells, misfit, sems):
    own = pl.ds(BASE, ROWS)
    small = [
        pltpu.make_async_copy(heights_hbm, heights, sems.at[2, 1]),
        pltpu.make_async_copy(cells_hbm, cells, sems.at[2, 2]),
        pltpu.make_async_copy(misfit_hbm, misfit, sems.at[2, 3]),
    ]
    for copy in small:
        copy.start()
    load_rho = pltpu.make_async_copy(density, rho, sems.at[2, 0])
    load_rho.start()

    def load(tile):
        at = pl.ds(pl.multiple_of(tile * 128, 128), 128)
        return (
            pltpu.make_async_copy(adjoint.at[:, :, at], field.at[tile, :, own, :], sems.at[0, tile]),
            pltpu.make_async_copy(velocity.at[:, :, :, at], u.at[tile, :, :, own, :], sems.at[1, tile]),
        )

    def arrived(tile):
        for copy in load(tile):
            copy.wait()

    for tile in range(TILES):
        for copy in load(tile):
            copy.start()
    geo = Geometry()
    for copy in small:
        copy.wait()
    tall[BASE : BASE + ROWS, 0:COLS] = heights[...].astype(F32)
    for tile in range(TILES):
        for row in range(BASE, BASE + ROWS, 8):
            tops[0, tile, row : row + 8] = column_tops(tall, tile, row)
    for tile in range(1, TILES - 1):
        for row in range(BASE, BASE + ROWS, 8):
            shifted_tops(geo, tops, tile, row)

    numbers = cells[0]
    row = numbers // (COLS * NZ)
    lane = numbers % (COLS * NZ)
    here = lax.broadcasted_iota(jnp.int32, (ROWS, SENS), 0) == row
    parts = []
    for back in range(2):
        for axis in range(3):
            parts.append(split(jnp.where(here, SCALES[back][1] * misfit[back, axis, 0], 0.0)))
    left = jnp.concatenate(
        [jnp.concatenate([part[index] for part in parts], axis=0) for index in range(2)], axis=1
    )
    load_rho.wait()
    for pair in range(TILES // 2):
        right = one_hot(lane, 2 * pair, 256)
        summed = product(left, jnp.concatenate([right, right], axis=1))
        for half in range(2):
            tile = 2 * pair + half
            at = pl.ds(tile * 128, 128)
            for back in range(2):
                inverse = 1.0 / rho[back, :, at]
                for axis in range(3):
                    first = (3 * back + axis) * ROWS
                    force[tile, back, axis, own, :] = (
                        summed[first : first + ROWS, 128 * half : 128 * half + 128] * inverse
                    )
    arrived(0)
    arrived(1)

    def inner(tile, carry):
        arrived(tile + 1)
        step(geo, 1, field, middle, u, force, tops, STARTS_INNER, tile, tile + 1, tile - 1)
        return carry

    lax.fori_loop(1, TILES - 1, inner, 0)


def prepare(adjoint, velocity, density, heights, cells, misfit):
    return pl.pallas_call(
        prepare_kernel,
        out_shape=(FIELD, FIELD, VECTORS, VECTORS, TOPS, TALL),
        in_specs=[HBM] * 6,
        out_specs=(VMEM,) * 6,
        scratch_shapes=[
            pltpu.VMEM((2, ROWS, TILES * 128), F32),
            pltpu.VMEM((ROWS, COLS), jnp.int32),
            pltpu.VMEM((1, 1, SENS), jnp.int32),
            pltpu.VMEM((2, 3, 1, 1, SENS), F32),
            pltpu.SemaphoreType.DMA((3, TILES)),
        ],
        compiler_params=pltpu.CompilerParams(vmem_limit_bytes=PREPARE_VMEM),
        cost_estimate=pl.CostEstimate(flops=40_000_000, bytes_accessed=8_000_000, transcendentals=0),
        name="prepare",
    )(adjoint, velocity, density, heights, cells, misfit)


def pack_y_kernel(own_tall, all_field, all_u, all_force, msg_a, msg_b,
                  out_a, out_b, field, u, force, tall, tops, partial):
    slots = ((0, 0), (1, TILES - 1))
    own = pl.ds(BASE, ROWS)
    for slot, tile in slots:
        field[slot, :, own, :] = all_field[tile, :, own, :]
        u[slot, 1, :, own, :] = all_u[tile, 1, :, own, :]
        force[slot, 1, :, own, :] = all_force[tile, 1, :, own, :]
    tall[BASE : BASE + ROWS] = own_tall[BASE : BASE + ROWS]
    geo = Geometry()

    def from_x(low_msg, high_msg):
        for message, side in ((low_msg, "lo"), (high_msg, "hi")):
            place_tall(message, side, tall)
            for slot, tile in slots:
                place_x(message, side, slot, tile, field, u, force)

    by_parity(lax.axis_index("gx") % 2, lambda: from_x(msg_a, msg_b), lambda: from_x(msg_b, msg_a))
    for slot, tile in slots:
        for row in range(0, EXT, 8):
            value = column_tops(tall, tile, row)
            tops[slot, 0, row : row + 8] = value
            tops[slot, 1, row : row + 8] = half_turn(value)

    def read(tile, number, row):
        return field[tile, number, pl.ds(row, 8), :]

    for slot, side in ((0, "lo"), (1, "hi")):
        inward = 1 if side == "lo" else -1
        numbers = [n for n in range(K) if VELOCITIES[n][1] in (0, inward)]
        for start in STARTS_WIDE:
            at = pl.ds(start, 8)

            def top(cy, row, slot=slot):
                return tops[slot, 0 if cy == 0 else 1, pl.ds(row, 8), :]

            f = incoming(geo, read, top, slot, slot, slot, start, numbers)
            velocity_here = [u[slot, 1, axis, at, :] for axis in range(3)]
            push = [force[slot, 1, axis, at, :] for axis in range(3)]
            result = collide(f, velocity_here, push, Y_SIDE[side], 1)
            for index, number in enumerate(Y_SIDE[side]):
                partial[slot, index, at, :] = result[number]

    def write(side, out):
        slot = 0 if side == "lo" else 1
        for start in range(0, 40, 8):
            at = pl.ds(start + BASE - 2, 8)
            pairs = [
                (field[slot, number, at, :], partial[slot, index, at, :])
                for index, number in enumerate(Y_SIDE[side])
            ]
            pairs.append((u[slot, 1, 0, at, :], u[slot, 1, 1, at, :]))
            pairs.append((u[slot, 1, 2, at, :], tops[slot, 0, at, :]))
            for index, (first, second) in enumerate(pairs):
                turned = half_turn(second)
                if side == "lo":
                    value = jnp.where(geo.low, first, turned)
                else:
                    value = jnp.where(geo.low, turned, first)
                out[index, start : start + 8, :] = value

    def upper():
        write("hi", out_a)
        write("lo", out_b)

    def lower():
        write("lo", out_a)
        write("hi", out_b)

    by_parity(lax.axis_index("gy") % 2, upper, lower)


def pack_y(heights, field, u, force, msg_a, msg_b):
    shape = jax.ShapeDtypeStruct((Y_FIELDS, 40, 128), F32)
    return pl.pallas_call(
        pack_y_kernel,
        out_shape=(shape, shape),
        in_specs=[VMEM] * 6,
        out_specs=(VMEM, VMEM),
        scratch_shapes=[
            pltpu.VMEM((2, K, EXT, 128), F32),
            pltpu.VMEM((2, 2, 3, EXT, 128), F32),
            pltpu.VMEM((2, 2, 3, EXT, 128), F32),
            pltpu.VMEM((EXT, 128), F32),
            pltpu.VMEM((2, 2, EXT, 128), F32),
            pltpu.VMEM((2, 5, EXT, 128), F32),
        ],
        compiler_params=pltpu.CompilerParams(vmem_limit_bytes=SMALL_VMEM),
        name="pack_y",
    )(heights, field, u, force, msg_a, msg_b)


def send_out(field, out, sems, tile):
    at = pl.ds(pl.multiple_of(tile * 128, 128), 128)
    return pltpu.make_async_copy(field.at[tile, :, pl.ds(BASE, ROWS), :], out.at[:, :, at], sems.at[tile])


def inner_kernel(own_tall, msg_a, msg_b, order, field_in, middle_in, u_in, force_in, tops_in,
                 field, middle, u, force, tops, out, tall, sems):
    del order, field_in, middle_in, u_in, force_in, tops_in
    geo = Geometry()
    tall[BASE : BASE + ROWS] = own_tall[BASE : BASE + ROWS]

    def from_x(low_msg, high_msg):
        for message, side in ((low_msg, "lo"), (high_msg, "hi")):
            place_tall(message, side, tall)
            for tile in range(TILES):
                place_x(message, side, tile, tile, field, u, force)

    by_parity(lax.axis_index("gx") % 2, lambda: from_x(msg_a, msg_b), lambda: from_x(msg_b, msg_a))
    for tile in range(TILES):
        for row in (0, BASE + ROWS):
            tops[0, tile, row : row + 8] = column_tops(tall, tile, row)
    for tile in range(1, TILES - 1):
        for row in (0, BASE + ROWS):
            shifted_tops(geo, tops, tile, row)

    def edges(tile):
        step(geo, 1, field, middle, u, force, tops, STARTS_EDGE, tile, tile + 1, tile - 1)

    edges(1)
    edges(2)

    def second(tile, carry):
        edges(tile + 1)
        step(geo, 0, middle, field, u, force, tops, STARTS_OWN, tile, tile + 1, tile - 1)
        send_out(field, out, sems, tile).start()
        return carry

    def sent(tile, carry):
        send_out(field, out, sems, tile).wait()
        return carry

    lax.fori_loop(2, TILES - 2, second, 0)
    lax.fori_loop(2, TILES - 2, sent, 0)


def inner_columns(heights, msg_a, msg_b, order, field, middle, u, force, tops, shape):
    return pl.pallas_call(
        inner_kernel,
        out_shape=(FIELD, FIELD, VECTORS, VECTORS, TOPS, jax.ShapeDtypeStruct(shape, F32)),
        in_specs=[VMEM] * 3 + [HBM] + [VMEM] * 5,
        out_specs=(VMEM,) * 5 + (HBM,),
        input_output_aliases={4: 0, 5: 1, 6: 2, 7: 3, 8: 4},
        scratch_shapes=[pltpu.VMEM((EXT, 128), F32), pltpu.SemaphoreType.DMA((TILES,))],
        compiler_params=pltpu.CompilerParams(vmem_limit_bytes=SMALL_VMEM),
        cost_estimate=pl.CostEstimate(flops=40_000_000, bytes_accessed=8_000_000, transcendentals=0),
        name="inner_columns",
    )(heights, msg_a, msg_b, order, field, middle, u, force, tops)


def outer_kernel(msg_a, msg_b, field_in, middle_in, u, force, tops_in, out_in,
                 field, middle, tops, out, side_partial, side_u, sems):
    del field_in, middle_in, tops_in, out_in
    geo = Geometry()

    def from_y(low_msg, high_msg):
        for start in range(0, 40, 8):
            at = pl.ds(start + BASE - 2, 8)
            for index in range(Y_FIELDS):
                low_value = low_msg[index, start : start + 8, :]
                high_value = high_msg[index, start : start + 8, :]
                low_turned, high_turned = half_turn(low_value), half_turn(high_value)
                if index < 5:
                    field[TILES, Y_SIDE["lo"][index], at, :] = low_value
                    field[TILES, Y_SIDE["hi"][index], at, :] = high_value
                    side_partial[0, index, at, :] = low_turned
                    side_partial[1, index, at, :] = high_turned
                else:
                    first = jnp.where(geo.low, low_value, high_value)
                    second = jnp.where(geo.low, low_turned, high_turned)
                    if index == 5:
                        side_u[0, at, :] = first
                        side_u[1, at, :] = second
                    else:
                        side_u[2, at, :] = first
                        tops[0, TILES, at, :] = second

    by_parity(lax.axis_index("gy") % 2, lambda: from_y(msg_a, msg_b), lambda: from_y(msg_b, msg_a))
    for tile in (0, TILES - 1, TILES):
        for row in range(0, EXT, 8):
            shifted_tops(geo, tops, tile, row)
    for tile, after, before in ((0, 1, TILES), (TILES - 1, TILES, TILES - 2)):
        step(geo, 1, field, middle, u, force, tops, STARTS_WIDE, tile, after, before)

    def read(where, number, row):
        return field[where, number, pl.ds(row, 8), :]

    def top(cy, row):
        return tops[cy % 3, TILES, pl.ds(row, 8), :]

    for slot, side, other in ((0, "lo", "hi"), (1, "hi", "lo")):
        for start in STARTS_WIDE:
            at = pl.ds(start, 8)
            f = incoming(geo, read, top, TILES, 0, TILES - 1, start, Y_SIDE[other])
            velocity = [side_u[axis, at, :] for axis in range(3)]
            result = collide(f, velocity, None, Y_SIDE[side], 1)
            for index, number in enumerate(Y_SIDE[side]):
                middle[TILES, number, at, :] = result[number] + side_partial[slot, index, at, :]

    last = (1, TILES - 2, 0, TILES - 1)
    for tile in last:
        before = TILES if tile == 0 else tile - 1
        step(geo, 0, middle, field, u, force, tops, STARTS_OWN, tile, tile + 1, before)
        send_out(field, out, sems, tile).start()
    for tile in last:
        send_out(field, out, sems, tile).wait()


def outer_columns(msg_a, msg_b, field, middle, u, force, tops, out):
    return pl.pallas_call(
        outer_kernel,
        out_shape=(FIELD, FIELD, TOPS, jax.ShapeDtypeStruct(out.shape, F32)),
        in_specs=[VMEM] * 7 + [HBM],
        out_specs=(VMEM,) * 3 + (HBM,),
        input_output_aliases={2: 0, 3: 1, 6: 2, 7: 3},
        scratch_shapes=[
            pltpu.VMEM((2, 5, EXT, 128), F32),
            pltpu.VMEM((3, EXT, 128), F32),
            pltpu.SemaphoreType.DMA((TILES,)),
        ],
        compiler_params=pltpu.CompilerParams(vmem_limit_bytes=SMALL_VMEM),
        name="outer_columns",
    )(msg_a, msg_b, field, middle, u, force, tops, out)


def partners(count, odd):
    if not odd:
        return [(i, i ^ 1) for i in range(count)]
    return [(i, (i - 1) % count if i % 2 == 0 else (i + 1) % count) for i in range(count)]


def swap(value, axis, odd):
    return lax.ppermute(value, axis, partners(lax.axis_size(axis), odd))


def per_device(adjoint, velocity, density, heights, cells, misfit):
    args = [
        pltpu.with_memory_space_constraint(value, pltpu.HBM)
        for value in (adjoint, velocity, density, heights, cells, misfit)
    ]
    x_a, x_b = pack_x(*args)
    x_a, x_b = swap(x_a, "gx", True), swap(x_b, "gx", False)
    field, middle, u, force, tops, tall = prepare(*args)
    own_a, own_b = pack_y(tall, field, u, force, x_a, x_b)
    y_a, y_b = swap(own_a, "gy", True), swap(own_b, "gy", False)
    field, middle, u, force, tops, out = inner_columns(
        tall, x_a, x_b, own_a, field, middle, u, force, tops, adjoint.shape
    )
    return outer_columns(y_a, y_b, field, middle, u, force, tops, out)[3]


def solution(mesh):
    return jax.shard_map(
        per_device,
        mesh=mesh,
        in_specs=(
            P(None, "gx", "gy"),
            P(None, None, "gx", "gy"),
            P(None, "gx", "gy"),
            P("gx", "gy"),
            P("gx", "gy", None),
            P(None, None, "gx", "gy", None),
        ),
        out_specs=P(None, "gx", "gy"),
        check_vma=False,
    )
```

```python
import functools

import jax
import jax.numpy as jnp
from jax import lax
from jax.experimental import pallas as pl
from jax.experimental.pallas import tpu as pltpu
from jax.sharding import PartitionSpec as P

VELOCITIES = (
    (0, 0, 0),
    (1, 0, 0),
    (-1, 0, 0),
    (0, 1, 0),
    (0, -1, 0),
    (0, 0, 1),
    (0, 0, -1),
    (1, 1, 0),
    (-1, -1, 0),
    (1, -1, 0),
    (-1, 1, 0),
    (1, 0, 1),
    (-1, 0, -1),
    (1, 0, -1),
    (-1, 0, 1),
    (0, 1, 1),
    (0, -1, -1),
    (0, 1, -1),
    (0, -1, 1),
)
OPPOSITE = (0, 2, 1, 4, 3, 6, 5, 8, 7, 10, 9, 12, 11, 14, 13, 16, 15, 18, 17)
K = 19
ROWS, COLS, NZ = 32, 32, 64
TILES = COLS * NZ // 128
EXT = 48
BASE = 8
SENS = 128
STARTS_WIDE = (7, 15, 23, 31, 33)
STARTS_OWN = (8, 16, 24, 32)
STARTS_INNER = (9, 17, 25, 31)
STARTS_EDGE = (7, 33)
X_SIDE = {"lo": (1, 7, 9, 11, 13), "hi": (2, 8, 10, 12, 14)}
Y_SIDE = {"lo": (3, 7, 10, 15, 17), "hi": (4, 8, 9, 16, 18)}
X_FIELDS = 32
Y_FIELDS = 7
F32 = jnp.float32
MB = 1024 * 1024
PREPARE_VMEM = 4 * MB
SMALL_VMEM = 4 * MB
HBM = pl.BlockSpec(memory_space=pltpu.HBM)
VMEM = pl.BlockSpec(memory_space=pltpu.VMEM)


def add(a, b):
    if a is None:
        return b
    return a if b is None else a + b


def sub(a, b):
    if b is None:
        return a
    return -b if a is None else a - b


def lanes():
    return lax.broadcasted_iota(jnp.int32, (8, 128), 1)


class Geometry:
    def __init__(self):
        lane = lanes()
        level = lane % NZ
        self.low = lane < NZ
        self.level = level.astype(F32)
        up = jnp.where(level == NZ - 1, -1, level + 1).astype(F32)
        self.raised = {0: self.level, 1: up, -1: self.level - 1.0}


def half_turn(value):
    return pltpu.roll(value, NZ, 1)


def from_next(geo, here, after):
    return jnp.where(geo.low, after, here)


def from_previous(geo, here, before):
    return jnp.where(geo.low, here, before)


def pull(geo, read, tile, after, before, position, number):
    cx, cy, cz = VELOCITIES[number]
    row = position + cx
    if cy == 0:
        value = read(tile, number, row)
        return pltpu.roll(value, (128 - cz) % 128, 1) if cz else value
    if cy == 1:
        value = from_next(geo, read(tile, number, row), read(after, number, row))
    else:
        value = from_previous(geo, read(tile, number, row), read(before, number, row))
    return pltpu.roll(value, NZ - cz, 1)


def incoming(geo, read, tops, tile, after, before, position, numbers):
    out = [None] * K
    for number in numbers:
        cx, cy, cz = VELOCITIES[number]
        value = pull(geo, read, tile, after, before, position, number)
        if number:
            blocked = geo.raised[cz] < tops(cy, position + cx)
            value = jnp.where(blocked, read(tile, OPPOSITE[number], position), value)
        out[number] = value
    return out


def moments(f):
    plus = [None] * K
    minus = [None] * K
    for number in range(1, K, 2):
        plus[number] = add(f[number], f[number + 1])
        minus[number] = sub(f[number], f[number + 1])
    sxy, dxy = add(plus[7], plus[9]), sub(plus[7], plus[9])
    sxz, dxz = add(plus[11], plus[13]), sub(plus[11], plus[13])
    syz, dyz = add(plus[15], plus[17]), sub(plus[15], plus[17])
    twice = [None if plus[n] is None else plus[n] + plus[n] for n in (1, 3, 5)]
    mxx = add(twice[0], add(sxy, sxz))
    myy = add(twice[1], add(sxy, syz))
    mzz = add(twice[2], add(sxz, syz))
    total = add(add(add(twice[0], twice[1]), twice[2]), add(add(sxy, sxz), syz))
    if f[0] is not None:
        total = add(12.0 * f[0], total)

    def axis(main, first, second):
        doubled = None if minus[main] is None else minus[main] + minus[main]
        return add(doubled, add(first, second))

    jx = axis(1, add(minus[7], minus[9]), add(minus[11], minus[13]))
    jy = axis(3, sub(minus[7], minus[9]), add(minus[15], minus[17]))
    jz = axis(5, sub(minus[11], minus[13]), sub(minus[15], minus[17]))
    return total, (jx, jy, jz), (mxx, myy, mzz, dxy, dxz, dyz)


def mul(a, b):
    return None if a is None else a * b


SCALES = {1: (1.0, -1.25), 0: (-0.8, 1.0)}


def collide(f, u, force, numbers, number_of_step):
    read_scale, write_scale = SCALES[number_of_step]
    scale = read_scale * write_scale
    total, (jx, jy, jz), (mxx, myy, mzz, dxy, dxz, dyz) = moments(f)
    ux, uy, uz = u
    sx, sy, sz = (0.225 * scale) * ux, (0.225 * scale) * uy, (0.225 * scale) * uz
    qx = add(add(mul(mxx, sx), mul(dxy, sy)), mul(dxz, sz))
    qy = add(add(mul(dxy, sx), mul(myy, sy)), mul(dyz, sz))
    qz = add(add(mul(dxz, sx), mul(dyz, sy)), mul(mzz, sz))
    q = (qx, qy, qz)
    pushed = q if force is None else [q[axis] + force[axis] for axis in range(3)]
    speed = ux * ux + uy * uy + uz * uz
    scalar = total * (0.05 * scale + (0.075 * scale) * speed)
    scalar = scalar - (ux * pushed[0] + uy * pushed[1] + uz * pushed[2])
    scaled = (0.15 * scale) * total
    vector = []
    for axis, j in enumerate((jx, jy, jz)):
        value = q[axis] + pushed[axis] - scaled * u[axis]
        vector.append(add(mul(j, 0.15 * scale), value))
    out = {}
    along = {}
    for number in numbers:
        pair = number if number % 2 else number - 1
        if number == 0:
            value = scalar
        else:
            if pair not in along:
                first = VELOCITIES[pair]
                cv = None
                for axis in range(3):
                    if first[axis] == 1:
                        cv = add(cv, vector[axis])
                    elif first[axis] == -1:
                        cv = sub(cv, vector[axis])
                along[pair] = cv
            value = scalar + along[pair] if number == pair else scalar - along[pair]
        if f[number] is not None:
            value = value + (f[number] if number_of_step == 1 else (-0.8 * scale) * f[number])
        out[number] = value
    return out


def split(value):
    high = value.astype(jnp.bfloat16)
    return high, (value - high.astype(F32)).astype(jnp.bfloat16)


def one_hot(lane, tile, width):
    cells = lax.broadcasted_iota(jnp.int32, (width, SENS), 0) + tile * 128
    return jnp.where(cells == lane, 1.0, 0.0).astype(jnp.bfloat16)


def product(left, right):
    return lax.dot_general(left, right, (((1,), (1,)), ((), ())), preferred_element_type=F32)


def by_parity(parity, upper, lower):
    pl.when(parity == 1)(upper)
    pl.when(parity == 0)(lower)


def pack_x_kernel(adjoint, velocity, density, heights_hbm, cells_hbm, misfit_hbm, out_a, out_b,
                  rows_buf, u_buf, rho_buf, heights, cells, misfit, edge_force, sems):
    copies = [
        pltpu.make_async_copy(heights_hbm, heights, sems.at[2, 0]),
        pltpu.make_async_copy(cells_hbm, cells, sems.at[2, 1]),
        pltpu.make_async_copy(misfit_hbm, misfit, sems.at[2, 2]),
    ]
    for side, start in ((0, 0), (1, ROWS - 8)):
        for tile in range(TILES):
            at = pl.ds(tile * 128, 128)
            copies.append(
                pltpu.make_async_copy(adjoint.at[:, pl.ds(start, 8), at], rows_buf.at[side, tile], sems.at[side, tile])
            )
        copies.append(pltpu.make_async_copy(velocity.at[1, :, pl.ds(start, 8), :], u_buf.at[side], sems.at[side, TILES]))
        copies.append(pltpu.make_async_copy(density.at[1, pl.ds(start, 8), :], rho_buf.at[side], sems.at[side, TILES + 1]))
    for copy in copies:
        copy.start()
    for copy in copies[:3]:
        copy.wait()
    numbers = cells[0]
    lane = numbers % (COLS * NZ)
    parts = []
    for edge in (0, ROWS - 1):
        here = numbers // (COLS * NZ) == edge
        rows = [jnp.where(here, SCALES[1][1] * misfit[1, axis, 0], 0.0) for axis in range(3)]
        parts.append(split(jnp.concatenate(rows + [jnp.zeros((5, SENS), F32)], axis=0)))
    left = jnp.concatenate(
        [jnp.concatenate([part[index] for part in parts], axis=0) for index in range(2)], axis=1
    )
    for pair in range(TILES // 2):
        right = one_hot(lane, 2 * pair, 256)
        edge_force[:, pl.ds(256 * pair, 256)] = product(left, jnp.concatenate([right, right], axis=1))
    for copy in copies[3:]:
        copy.wait()
    flat = rows_buf.reshape(2, TILES, K * 8, 128)

    def pack(side, out):
        slot = 0 if side == "lo" else 1
        first = 0 if side == "lo" else 7
        second = 1 if side == "lo" else 6
        for tile in range(TILES):
            at = pl.ds(tile * 128, 128)
            out[0:8, at] = flat[slot, tile, pl.ds(first, 8, stride=8), :]
            out[8:16, at] = flat[slot, tile, pl.ds(64 + first, 8, stride=8), :]
            out[16:19, at] = flat[slot, tile, pl.ds(128 + first, 3, stride=8), :]
            for index, number in enumerate(X_SIDE[side]):
                out[19 + index : 20 + index, at] = rows_buf[slot, tile, number, second : second + 1, :]
        inverse = 1.0 / rho_buf[slot, first : first + 1, :]
        out[24:27, :] = edge_force[8 * slot : 8 * slot + 3, :] * inverse
        for axis in range(3):
            out[27 + axis : 28 + axis, :] = u_buf[slot, axis, first : first + 1, :]
        edge = 0 if side == "lo" else ROWS - 1
        inner = 1 if side == "lo" else ROWS - 2
        out[30:31, 0:COLS] = heights[edge : edge + 1, :].astype(F32)
        out[30:31, 128 : 128 + COLS] = heights[inner : inner + 1, :].astype(F32)

    def upper():
        pack("hi", out_a)
        pack("lo", out_b)

    def lower():
        pack("lo", out_a)
        pack("hi", out_b)

    by_parity(1 - lax.axis_index("gx") % 2, upper, lower)


def pack_x(adjoint, velocity, density, heights, cells, misfit):
    shape = jax.ShapeDtypeStruct((X_FIELDS, TILES * 128), F32)
    return pl.pallas_call(
        pack_x_kernel,
        out_shape=(shape, shape),
        in_specs=[HBM] * 6,
        out_specs=(VMEM, VMEM),
        scratch_shapes=[
            pltpu.VMEM((2, TILES, K, 8, 128), F32),
            pltpu.VMEM((2, 3, 8, TILES * 128), F32),
            pltpu.VMEM((2, 8, TILES * 128), F32),
            pltpu.VMEM((ROWS, COLS), jnp.int32),
            pltpu.VMEM((1, 1, SENS), jnp.int32),
            pltpu.VMEM((2, 3, 1, 1, SENS), F32),
            pltpu.VMEM((16, TILES * 128), F32),
            pltpu.SemaphoreType.DMA((3, TILES + 2)),
        ],
        compiler_params=pltpu.CompilerParams(vmem_limit_bytes=8 * MB),
        name="pack_x",
    )(adjoint, velocity, density, heights, cells, misfit)


def place_x(message, side, slot, tile, field, u, force):
    outer, inner = (BASE + ROWS, BASE + ROWS + 1) if side == "lo" else (BASE - 1, BASE - 2)
    flat = field.reshape(field.shape[0], K * EXT, 128)
    at = pl.ds(tile * 128, 128)
    flat[slot, pl.ds(outer, 8, stride=EXT), :] = message[0:8, at]
    flat[slot, pl.ds(8 * EXT + outer, 8, stride=EXT), :] = message[8:16, at]
    flat[slot, pl.ds(16 * EXT + outer, 3, stride=EXT), :] = message[16:19, at]
    for index, number in enumerate(X_SIDE[side]):
        field[slot, number, inner : inner + 1, :] = message[19 + index : 20 + index, at]
    for axis in range(3):
        force[slot, 1, axis, outer : outer + 1, :] = message[24 + axis : 25 + axis, at]
        u[slot, 1, axis, outer : outer + 1, :] = message[27 + axis : 28 + axis, at]


def place_tall(message, side, tall):
    outer, inner = (BASE + ROWS, BASE + ROWS + 1) if side == "lo" else (BASE - 1, BASE - 2)
    tall[outer : outer + 1, 0:COLS] = message[30:31, 0:COLS]
    tall[inner : inner + 1, 0:COLS] = message[30:31, 128 : 128 + COLS]


def column_tops(tall, tile, rows):
    at = slice(rows, rows + 8)
    low = lanes() < NZ
    left = jnp.broadcast_to(tall[at, 2 * tile : 2 * tile + 1], (8, 128))
    right = jnp.broadcast_to(tall[at, 2 * tile + 1 : 2 * tile + 2], (8, 128))
    return jnp.where(low, left, right)


def shifted_tops(geo, tops, tile, rows):
    at = pl.ds(rows, 8)
    after, before = (tile + 1) % (TILES + 1), (tile - 1) % (TILES + 1)
    here = tops[0, tile, at, :]
    tops[1, tile, at, :] = half_turn(from_next(geo, here, tops[0, after, at, :]))
    tops[2, tile, at, :] = half_turn(from_previous(geo, here, tops[0, before, at, :]))


def step(geo, number_of_step, source, target, u, force, tops, starts, tile, after, before):
    def read(where, number, row):
        return source[where, number, pl.ds(row, 8), :]

    def top(cy, row):
        return tops[cy % 3, tile, pl.ds(row, 8), :]

    for start in starts:
        at = pl.ds(start, 8)
        f = incoming(geo, read, top, tile, after, before, start, range(K))
        velocity = [u[tile, number_of_step, axis, at, :] for axis in range(3)]
        push = [force[tile, number_of_step, axis, at, :] for axis in range(3)]
        result = collide(f, velocity, push, range(K), number_of_step)
        if number_of_step:
            for number in range(K):
                target[tile, number, at, :] = result[number]
        else:
            fluid = geo.level >= tops[0, tile, at, :]
            for number in range(K):
                target[tile, number, at, :] = jnp.zeros((8, 128), F32)
                pltpu.store(target.at[tile, number, at, :], result[number], mask=fluid)


WIDE = TILES + 1
SENT_EARLY = 10
FIELD = jax.ShapeDtypeStruct((WIDE, K, EXT, 128), F32)
VECTORS = jax.ShapeDtypeStruct((TILES, 2, 3, EXT, 128), F32)
TOPS = jax.ShapeDtypeStruct((3, WIDE, EXT, 128), F32)
TALL = jax.ShapeDtypeStruct((EXT, 128), F32)


def prepare_kernel(adjoint, velocity, density, heights_hbm, cells_hbm, misfit_hbm,
                   field, middle, u, force, tops, tall, rho, heights, cells, misfit, sems):
    own = pl.ds(BASE, ROWS)
    small = [
        pltpu.make_async_copy(heights_hbm, heights, sems.at[2, 1]),
        pltpu.make_async_copy(cells_hbm, cells, sems.at[2, 2]),
        pltpu.make_async_copy(misfit_hbm, misfit, sems.at[2, 3]),
    ]
    for copy in small:
        copy.start()
    load_rho = pltpu.make_async_copy(density, rho, sems.at[2, 0])
    load_rho.start()

    def load(tile):
        at = pl.ds(pl.multiple_of(tile * 128, 128), 128)
        return (
            pltpu.make_async_copy(adjoint.at[:, :, at], field.at[tile, :, own, :], sems.at[0, tile]),
            pltpu.make_async_copy(velocity.at[:, :, :, at], u.at[tile, :, :, own, :], sems.at[1, tile]),
        )

    def arrived(tile):
        for copy in load(tile):
            copy.wait()

    for tile in range(TILES):
        for copy in load(tile):
            copy.start()
    geo = Geometry()
    for copy in small:
        copy.wait()
    tall[BASE : BASE + ROWS, 0:COLS] = heights[...].astype(F32)
    for tile in range(TILES):
        for row in range(BASE, BASE + ROWS, 8):
            tops[0, tile, row : row + 8] = column_tops(tall, tile, row)
    for tile in range(1, TILES - 1):
        for row in range(BASE, BASE + ROWS, 8):
            shifted_tops(geo, tops, tile, row)

    numbers = cells[0]
    row = numbers // (COLS * NZ)
    lane = numbers % (COLS * NZ)
    here = lax.broadcasted_iota(jnp.int32, (ROWS, SENS), 0) == row
    parts = []
    for back in range(2):
        for axis in range(3):
            parts.append(split(jnp.where(here, SCALES[back][1] * misfit[back, axis, 0], 0.0)))
    left = jnp.concatenate(
        [jnp.concatenate([part[index] for part in parts], axis=0) for index in range(2)], axis=1
    )
    load_rho.wait()
    for pair in range(TILES // 2):
        right = one_hot(lane, 2 * pair, 256)
        summed = product(left, jnp.concatenate([right, right], axis=1))
        for half in range(2):
            tile = 2 * pair + half
            at = pl.ds(tile * 128, 128)
            for back in range(2):
                inverse = 1.0 / rho[back, :, at]
                for axis in range(3):
                    first = (3 * back + axis) * ROWS
                    force[tile, back, axis, own, :] = (
                        summed[first : first + ROWS, 128 * half : 128 * half + 128] * inverse
                    )
    arrived(0)
    arrived(1)

    def inner(tile, carry):
        arrived(tile + 1)
        step(geo, 1, field, middle, u, force, tops, STARTS_INNER, tile, tile + 1, tile - 1)
        return carry

    lax.fori_loop(1, TILES - 1, inner, 0)


def prepare(adjoint, velocity, density, heights, cells, misfit):
    return pl.pallas_call(
        prepare_kernel,
        out_shape=(FIELD, FIELD, VECTORS, VECTORS, TOPS, TALL),
        in_specs=[HBM] * 6,
        out_specs=(VMEM,) * 6,
        scratch_shapes=[
            pltpu.VMEM((2, ROWS, TILES * 128), F32),
            pltpu.VMEM((ROWS, COLS), jnp.int32),
            pltpu.VMEM((1, 1, SENS), jnp.int32),
            pltpu.VMEM((2, 3, 1, 1, SENS), F32),
            pltpu.SemaphoreType.DMA((3, TILES)),
        ],
        compiler_params=pltpu.CompilerParams(vmem_limit_bytes=PREPARE_VMEM),
        cost_estimate=pl.CostEstimate(flops=40_000_000, bytes_accessed=8_000_000, transcendentals=0),
        name="prepare",
    )(adjoint, velocity, density, heights, cells, misfit)


def pack_y_kernel(own_tall, all_field, all_u, all_force, msg_a, msg_b,
                  out_a, out_b, field, u, force, tall, tops, partial):
    slots = ((0, 0), (1, TILES - 1))
    own = pl.ds(BASE, ROWS)
    for slot, tile in slots:
        field[slot, :, own, :] = all_field[tile, :, own, :]
        u[slot, 1, :, own, :] = all_u[tile, 1, :, own, :]
        force[slot, 1, :, own, :] = all_force[tile, 1, :, own, :]
    tall[BASE : BASE + ROWS] = own_tall[BASE : BASE + ROWS]
    geo = Geometry()

    def from_x(low_msg, high_msg):
        for message, side in ((low_msg, "lo"), (high_msg, "hi")):
            place_tall(message, side, tall)
            for slot, tile in slots:
                place_x(message, side, slot, tile, field, u, force)

    by_parity(1 - lax.axis_index("gx") % 2, lambda: from_x(msg_a, msg_b), lambda: from_x(msg_b, msg_a))
    for slot, tile in slots:
        for row in range(0, EXT, 8):
            value = column_tops(tall, tile, row)
            tops[slot, 0, row : row + 8] = value
            tops[slot, 1, row : row + 8] = half_turn(value)

    def read(tile, number, row):
        return field[tile, number, pl.ds(row, 8), :]

    for slot, side in ((0, "lo"), (1, "hi")):
        inward = 1 if side == "lo" else -1
        numbers = [n for n in range(K) if VELOCITIES[n][1] in (0, inward)]
        for start in STARTS_WIDE:
            at = pl.ds(start, 8)

            def top(cy, row, slot=slot):
                return tops[slot, 0 if cy == 0 else 1, pl.ds(row, 8), :]

            f = incoming(geo, read, top, slot, slot, slot, start, numbers)
            velocity_here = [u[slot, 1, axis, at, :] for axis in range(3)]
            push = [force[slot, 1, axis, at, :] for axis in range(3)]
            result = collide(f, velocity_here, push, Y_SIDE[side], 1)
            for index, number in enumerate(Y_SIDE[side]):
                partial[slot, index, at, :] = result[number]

    def write(side, out):
        slot = 0 if side == "lo" else 1
        for start in range(0, 40, 8):
            at = pl.ds(start + BASE - 2, 8)
            pairs = [
                (field[slot, number, at, :], partial[slot, index, at, :])
                for index, number in enumerate(Y_SIDE[side])
            ]
            pairs.append((u[slot, 1, 0, at, :], u[slot, 1, 1, at, :]))
            pairs.append((u[slot, 1, 2, at, :], tops[slot, 0, at, :]))
            for index, (first, second) in enumerate(pairs):
                turned = half_turn(second)
                if side == "lo":
                    value = jnp.where(geo.low, first, turned)
                else:
                    value = jnp.where(geo.low, turned, first)
                out[index, start : start + 8, :] = value

    def upper():
        write("hi", out_a)
        write("lo", out_b)

    def lower():
        write("lo", out_a)
        write("hi", out_b)

    by_parity(lax.axis_index("gy") % 2, upper, lower)


def pack_y(heights, field, u, force, msg_a, msg_b):
    shape = jax.ShapeDtypeStruct((Y_FIELDS, 40, 128), F32)
    return pl.pallas_call(
        pack_y_kernel,
        out_shape=(shape, shape),
        in_specs=[VMEM] * 6,
        out_specs=(VMEM, VMEM),
        scratch_shapes=[
            pltpu.VMEM((2, K, EXT, 128), F32),
            pltpu.VMEM((2, 2, 3, EXT, 128), F32),
            pltpu.VMEM((2, 2, 3, EXT, 128), F32),
            pltpu.VMEM((EXT, 128), F32),
            pltpu.VMEM((2, 2, EXT, 128), F32),
            pltpu.VMEM((2, 5, EXT, 128), F32),
        ],
        compiler_params=pltpu.CompilerParams(vmem_limit_bytes=SMALL_VMEM),
        name="pack_y",
    )(heights, field, u, force, msg_a, msg_b)


def send_out(field, out, sems, tile):
    at = pl.ds(pl.multiple_of(tile * 128, 128), 128)
    return pltpu.make_async_copy(field.at[tile, :, pl.ds(BASE, ROWS), :], out.at[:, :, at], sems.at[tile])


def inner_kernel(own_tall, msg_a, msg_b, order, field_in, middle_in, u_in, force_in, tops_in,
                 field, middle, u, force, tops, out, tall, sems):
    del order, field_in, middle_in, u_in, force_in, tops_in
    geo = Geometry()
    tall[BASE : BASE + ROWS] = own_tall[BASE : BASE + ROWS]

    def from_x(low_msg, high_msg):
        for message, side in ((low_msg, "lo"), (high_msg, "hi")):
            place_tall(message, side, tall)
            for tile in range(TILES):
                place_x(message, side, tile, tile, field, u, force)

    by_parity(1 - lax.axis_index("gx") % 2, lambda: from_x(msg_a, msg_b), lambda: from_x(msg_b, msg_a))
    for tile in range(TILES):
        for row in (0, BASE + ROWS):
            tops[0, tile, row : row + 8] = column_tops(tall, tile, row)
    for tile in range(1, TILES - 1):
        for row in (0, BASE + ROWS):
            shifted_tops(geo, tops, tile, row)

    def edges(tile):
        step(geo, 1, field, middle, u, force, tops, STARTS_EDGE, tile, tile + 1, tile - 1)

    edges(1)
    edges(2)

    def second(tile, carry):
        edges(tile + 1)
        step(geo, 0, middle, field, u, force, tops, STARTS_OWN, tile, tile + 1, tile - 1)
        pl.when(tile < SENT_EARLY)(lambda: send_out(field, out, sems, tile).start())
        return carry

    def sent(tile, carry):
        send_out(field, out, sems, tile).wait()
        return carry

    lax.fori_loop(2, TILES - 2, second, 0)
    lax.fori_loop(2, SENT_EARLY, sent, 0)


def inner_columns(heights, msg_a, msg_b, order, field, middle, u, force, tops, shape):
    return pl.pallas_call(
        inner_kernel,
        out_shape=(FIELD, FIELD, VECTORS, VECTORS, TOPS, jax.ShapeDtypeStruct(shape, F32)),
        in_specs=[VMEM] * 3 + [HBM] + [VMEM] * 5,
        out_specs=(VMEM,) * 5 + (HBM,),
        input_output_aliases={4: 0, 5: 1, 6: 2, 7: 3, 8: 4},
        scratch_shapes=[pltpu.VMEM((EXT, 128), F32), pltpu.SemaphoreType.DMA((TILES,))],
        compiler_params=pltpu.CompilerParams(vmem_limit_bytes=SMALL_VMEM),
        cost_estimate=pl.CostEstimate(flops=40_000_000, bytes_accessed=8_000_000, transcendentals=0),
        name="inner_columns",
    )(heights, msg_a, msg_b, order, field, middle, u, force, tops)


def outer_kernel(msg_a, msg_b, field_in, middle_in, u, force, tops_in, out_in,
                 field, middle, tops, out, side_partial, side_u, sems):
    del field_in, middle_in, tops_in, out_in
    for tile in range(SENT_EARLY, TILES - 2):
        send_out(field, out, sems, tile).start()
    geo = Geometry()

    def from_y(low_msg, high_msg):
        for start in range(0, 40, 8):
            at = pl.ds(start + BASE - 2, 8)
            for index in range(Y_FIELDS):
                low_value = low_msg[index, start : start + 8, :]
                high_value = high_msg[index, start : start + 8, :]
                low_turned, high_turned = half_turn(low_value), half_turn(high_value)
                if index < 5:
                    field[TILES, Y_SIDE["lo"][index], at, :] = low_value
                    field[TILES, Y_SIDE["hi"][index], at, :] = high_value
                    side_partial[0, index, at, :] = low_turned
                    side_partial[1, index, at, :] = high_turned
                else:
                    first = jnp.where(geo.low, low_value, high_value)
                    second = jnp.where(geo.low, low_turned, high_turned)
                    if index == 5:
                        side_u[0, at, :] = first
                        side_u[1, at, :] = second
                    else:
                        side_u[2, at, :] = first
                        tops[0, TILES, at, :] = second

    by_parity(lax.axis_index("gy") % 2, lambda: from_y(msg_a, msg_b), lambda: from_y(msg_b, msg_a))
    for tile in (0, TILES - 1, TILES):
        for row in range(0, EXT, 8):
            shifted_tops(geo, tops, tile, row)
    for tile, after, before in ((0, 1, TILES), (TILES - 1, TILES, TILES - 2)):
        step(geo, 1, field, middle, u, force, tops, STARTS_WIDE, tile, after, before)

    def read(where, number, row):
        return field[where, number, pl.ds(row, 8), :]

    def top(cy, row):
        return tops[cy % 3, TILES, pl.ds(row, 8), :]

    for slot, side, other in ((0, "lo", "hi"), (1, "hi", "lo")):
        for start in STARTS_WIDE:
            at = pl.ds(start, 8)
            f = incoming(geo, read, top, TILES, 0, TILES - 1, start, Y_SIDE[other])
            velocity = [side_u[axis, at, :] for axis in range(3)]
            result = collide(f, velocity, None, Y_SIDE[side], 1)
            for index, number in enumerate(Y_SIDE[side]):
                middle[TILES, number, at, :] = result[number] + side_partial[slot, index, at, :]

    last = (1, TILES - 2, 0, TILES - 1)
    for tile in last:
        before = TILES if tile == 0 else tile - 1
        step(geo, 0, middle, field, u, force, tops, STARTS_OWN, tile, tile + 1, before)
        send_out(field, out, sems, tile).start()
    for tile in tuple(range(SENT_EARLY, TILES - 2)) + last:
        send_out(field, out, sems, tile).wait()


def outer_columns(msg_a, msg_b, field, middle, u, force, tops, out):
    return pl.pallas_call(
        outer_kernel,
        out_shape=(FIELD, FIELD, TOPS, jax.ShapeDtypeStruct(out.shape, F32)),
        in_specs=[VMEM] * 7 + [HBM],
        out_specs=(VMEM,) * 3 + (HBM,),
        input_output_aliases={2: 0, 3: 1, 6: 2, 7: 3},
        scratch_shapes=[
            pltpu.VMEM((2, 5, EXT, 128), F32),
            pltpu.VMEM((3, EXT, 128), F32),
            pltpu.SemaphoreType.DMA((TILES,)),
        ],
        compiler_params=pltpu.CompilerParams(vmem_limit_bytes=SMALL_VMEM),
        name="outer_columns",
    )(msg_a, msg_b, field, middle, u, force, tops, out)


def partners(count, odd):
    if not odd:
        return [(i, i ^ 1) for i in range(count)]
    return [(i, (i - 1) % count if i % 2 == 0 else (i + 1) % count) for i in range(count)]


def swap(value, axis, odd):
    return lax.ppermute(value, axis, partners(lax.axis_size(axis), odd))


def per_device(adjoint, velocity, density, heights, cells, misfit):
    args = [
        pltpu.with_memory_space_constraint(value, pltpu.HBM)
        for value in (adjoint, velocity, density, heights, cells, misfit)
    ]
    x_a, x_b = pack_x(*args)
    x_a, x_b = swap(x_a, "gx", False), swap(x_b, "gx", True)
    field, middle, u, force, tops, tall = prepare(*args)
    own_a, own_b = pack_y(tall, field, u, force, x_a, x_b)
    y_a, y_b = swap(own_a, "gy", True), swap(own_b, "gy", False)
    field, middle, u, force, tops, out = inner_columns(
        tall, x_a, x_b, own_a, field, middle, u, force, tops, adjoint.shape
    )
    return outer_columns(y_a, y_b, field, middle, u, force, tops, out)[3]


def solution(mesh):
    return jax.shard_map(
        per_device,
        mesh=mesh,
        in_specs=(
            P(None, "gx", "gy"),
            P(None, None, "gx", "gy"),
            P(None, "gx", "gy"),
            P("gx", "gy"),
            P("gx", "gy", None),
            P(None, None, "gx", "gy", None),
        ),
        out_specs=P(None, "gx", "gy"),
        check_vma=False,
    )
```

```python
import functools

import jax
import jax.numpy as jnp
from jax import lax
from jax.experimental import pallas as pl
from jax.experimental.pallas import tpu as pltpu
from jax.sharding import PartitionSpec as P

VELOCITIES = (
    (0, 0, 0),
    (1, 0, 0),
    (-1, 0, 0),
    (0, 1, 0),
    (0, -1, 0),
    (0, 0, 1),
    (0, 0, -1),
    (1, 1, 0),
    (-1, -1, 0),
    (1, -1, 0),
    (-1, 1, 0),
    (1, 0, 1),
    (-1, 0, -1),
    (1, 0, -1),
    (-1, 0, 1),
    (0, 1, 1),
    (0, -1, -1),
    (0, 1, -1),
    (0, -1, 1),
)
OPPOSITE = (0, 2, 1, 4, 3, 6, 5, 8, 7, 10, 9, 12, 11, 14, 13, 16, 15, 18, 17)
K = 19
ROWS, COLS, NZ = 32, 32, 64
TILES = COLS * NZ // 128
EXT = 48
BASE = 8
SENS = 128
STARTS_WIDE = (7, 15, 23, 31, 33)
STARTS_OWN = (8, 16, 24, 32)
STARTS_INNER = (9, 17, 25)
STARTS_EDGE = (7, 33)
X_SIDE = {"lo": (1, 7, 9, 11, 13), "hi": (2, 8, 10, 12, 14)}
Y_SIDE = {"lo": (3, 7, 10, 15, 17), "hi": (4, 8, 9, 16, 18)}
X_FIELDS = 32
Y_FIELDS = 7
F32 = jnp.float32
MB = 1024 * 1024
PREPARE_VMEM = 4 * MB
SMALL_VMEM = 4 * MB
HBM = pl.BlockSpec(memory_space=pltpu.HBM)
VMEM = pl.BlockSpec(memory_space=pltpu.VMEM)


def add(a, b):
    if a is None:
        return b
    return a if b is None else a + b


def sub(a, b):
    if b is None:
        return a
    return -b if a is None else a - b


def lanes():
    return lax.broadcasted_iota(jnp.int32, (8, 128), 1)


class Geometry:
    def __init__(self):
        lane = lanes()
        level = lane % NZ
        self.low = lane < NZ
        self.level = level.astype(F32)
        up = jnp.where(level == NZ - 1, -1, level + 1).astype(F32)
        self.raised = {0: self.level, 1: up, -1: self.level - 1.0}


def half_turn(value):
    return pltpu.roll(value, NZ, 1)


def from_next(geo, here, after):
    return jnp.where(geo.low, after, here)


def from_previous(geo, here, before):
    return jnp.where(geo.low, here, before)


def pull(geo, read, tile, after, before, position, number):
    cx, cy, cz = VELOCITIES[number]
    row = position + cx
    if cy == 0:
        value = read(tile, number, row)
        return pltpu.roll(value, (128 - cz) % 128, 1) if cz else value
    if cy == 1:
        value = from_next(geo, read(tile, number, row), read(after, number, row))
    else:
        value = from_previous(geo, read(tile, number, row), read(before, number, row))
    return pltpu.roll(value, NZ - cz, 1)


def incoming(geo, read, tops, tile, after, before, position, numbers):
    out = [None] * K
    for number in numbers:
        cx, cy, cz = VELOCITIES[number]
        value = pull(geo, read, tile, after, before, position, number)
        if number:
            blocked = geo.raised[cz] < tops(cy, position + cx)
            value = jnp.where(blocked, read(tile, OPPOSITE[number], position), value)
        out[number] = value
    return out


def moments(f):
    plus = [None] * K
    minus = [None] * K
    for number in range(1, K, 2):
        plus[number] = add(f[number], f[number + 1])
        minus[number] = sub(f[number], f[number + 1])
    sxy, dxy = add(plus[7], plus[9]), sub(plus[7], plus[9])
    sxz, dxz = add(plus[11], plus[13]), sub(plus[11], plus[13])
    syz, dyz = add(plus[15], plus[17]), sub(plus[15], plus[17])
    twice = [None if plus[n] is None else plus[n] + plus[n] for n in (1, 3, 5)]
    mxx = add(twice[0], add(sxy, sxz))
    myy = add(twice[1], add(sxy, syz))
    mzz = add(twice[2], add(sxz, syz))
    total = add(add(add(twice[0], twice[1]), twice[2]), add(add(sxy, sxz), syz))
    if f[0] is not None:
        total = add(12.0 * f[0], total)

    def axis(main, first, second):
        doubled = None if minus[main] is None else minus[main] + minus[main]
        return add(doubled, add(first, second))

    jx = axis(1, add(minus[7], minus[9]), add(minus[11], minus[13]))
    jy = axis(3, sub(minus[7], minus[9]), add(minus[15], minus[17]))
    jz = axis(5, sub(minus[11], minus[13]), sub(minus[15], minus[17]))
    return total, (jx, jy, jz), (mxx, myy, mzz, dxy, dxz, dyz)


def mul(a, b):
    return None if a is None else a * b


SCALES = {1: (1.0, -1.25), 0: (-0.8, 1.0)}


def collide(f, u, force, numbers, number_of_step):
    read_scale, write_scale = SCALES[number_of_step]
    scale = read_scale * write_scale
    total, (jx, jy, jz), (mxx, myy, mzz, dxy, dxz, dyz) = moments(f)
    ux, uy, uz = u
    sx, sy, sz = (0.225 * scale) * ux, (0.225 * scale) * uy, (0.225 * scale) * uz
    qx = add(add(mul(mxx, sx), mul(dxy, sy)), mul(dxz, sz))
    qy = add(add(mul(dxy, sx), mul(myy, sy)), mul(dyz, sz))
    qz = add(add(mul(dxz, sx), mul(dyz, sy)), mul(mzz, sz))
    q = (qx, qy, qz)
    pushed = q if force is None else [q[axis] + force[axis] for axis in range(3)]
    speed = ux * ux + uy * uy + uz * uz
    scalar = total * (0.05 * scale + (0.075 * scale) * speed)
    scalar = scalar - (ux * pushed[0] + uy * pushed[1] + uz * pushed[2])
    scaled = (0.15 * scale) * total
    vector = []
    for axis, j in enumerate((jx, jy, jz)):
        value = q[axis] + pushed[axis] - scaled * u[axis]
        vector.append(add(mul(j, 0.15 * scale), value))
    out = {}
    along = {}
    for number in numbers:
        pair = number if number % 2 else number - 1
        if number == 0:
            value = scalar
        else:
            if pair not in along:
                first = VELOCITIES[pair]
                cv = None
                for axis in range(3):
                    if first[axis] == 1:
                        cv = add(cv, vector[axis])
                    elif first[axis] == -1:
                        cv = sub(cv, vector[axis])
                along[pair] = cv
            value = scalar + along[pair] if number == pair else scalar - along[pair]
        if f[number] is not None:
            value = value + (f[number] if number_of_step == 1 else (-0.8 * scale) * f[number])
        out[number] = value
    return out


def split(value):
    high = value.astype(jnp.bfloat16)
    return high, (value - high.astype(F32)).astype(jnp.bfloat16)


def one_hot(lane, tile, width):
    cells = lax.broadcasted_iota(jnp.int32, (width, SENS), 0) + tile * 128
    return jnp.where(cells == lane, 1.0, 0.0).astype(jnp.bfloat16)


def product(left, right):
    return lax.dot_general(left, right, (((1,), (1,)), ((), ())), preferred_element_type=F32)


def by_parity(parity, upper, lower):
    pl.when(parity == 1)(upper)
    pl.when(parity == 0)(lower)


def pack_x_kernel(adjoint, velocity, density, heights_hbm, cells_hbm, misfit_hbm, out_a, out_b,
                  rows_buf, u_buf, rho_buf, heights, cells, misfit, edge_force, sems):
    copies = [
        pltpu.make_async_copy(heights_hbm, heights, sems.at[2, 0]),
        pltpu.make_async_copy(cells_hbm, cells, sems.at[2, 1]),
        pltpu.make_async_copy(misfit_hbm, misfit, sems.at[2, 2]),
    ]
    for side, start in ((0, 0), (1, ROWS - 8)):
        for tile in range(TILES):
            at = pl.ds(tile * 128, 128)
            copies.append(
                pltpu.make_async_copy(adjoint.at[:, pl.ds(start, 8), at], rows_buf.at[side, tile], sems.at[side, tile])
            )
        copies.append(pltpu.make_async_copy(velocity.at[1, :, pl.ds(start, 8), :], u_buf.at[side], sems.at[side, TILES]))
        copies.append(pltpu.make_async_copy(density.at[1, pl.ds(start, 8), :], rho_buf.at[side], sems.at[side, TILES + 1]))
    for copy in copies:
        copy.start()
    for copy in copies[:3]:
        copy.wait()
    numbers = cells[0]
    lane = numbers % (COLS * NZ)
    parts = []
    for edge in (0, ROWS - 1):
        here = numbers // (COLS * NZ) == edge
        rows = [jnp.where(here, SCALES[1][1] * misfit[1, axis, 0], 0.0) for axis in range(3)]
        parts.append(split(jnp.concatenate(rows + [jnp.zeros((5, SENS), F32)], axis=0)))
    left = jnp.concatenate(
        [jnp.concatenate([part[index] for part in parts], axis=0) for index in range(2)], axis=1
    )
    for pair in range(TILES // 2):
        right = one_hot(lane, 2 * pair, 256)
        edge_force[:, pl.ds(256 * pair, 256)] = product(left, jnp.concatenate([right, right], axis=1))
    for copy in copies[3:]:
        copy.wait()
    flat = rows_buf.reshape(2, TILES, K * 8, 128)

    def pack(side, out):
        slot = 0 if side == "lo" else 1
        first = 0 if side == "lo" else 7
        second = 1 if side == "lo" else 6
        for tile in range(TILES):
            at = pl.ds(tile * 128, 128)
            out[0:8, at] = flat[slot, tile, pl.ds(first, 8, stride=8), :]
            out[8:16, at] = flat[slot, tile, pl.ds(64 + first, 8, stride=8), :]
            out[16:19, at] = flat[slot, tile, pl.ds(128 + first, 3, stride=8), :]
            for index, number in enumerate(X_SIDE[side]):
                out[19 + index : 20 + index, at] = rows_buf[slot, tile, number, second : second + 1, :]
        inverse = 1.0 / rho_buf[slot, first : first + 1, :]
        out[24:27, :] = edge_force[8 * slot : 8 * slot + 3, :] * inverse
        for axis in range(3):
            out[27 + axis : 28 + axis, :] = u_buf[slot, axis, first : first + 1, :]
        edge = 0 if side == "lo" else ROWS - 1
        inner = 1 if side == "lo" else ROWS - 2
        out[30:31, 0:COLS] = heights[edge : edge + 1, :].astype(F32)
        out[30:31, 128 : 128 + COLS] = heights[inner : inner + 1, :].astype(F32)

    def upper():
        pack("hi", out_a)
        pack("lo", out_b)

    def lower():
        pack("lo", out_a)
        pack("hi", out_b)

    by_parity(1 - lax.axis_index("gx") % 2, upper, lower)


def pack_x(adjoint, velocity, density, heights, cells, misfit):
    shape = jax.ShapeDtypeStruct((X_FIELDS, TILES * 128), F32)
    return pl.pallas_call(
        pack_x_kernel,
        out_shape=(shape, shape),
        in_specs=[HBM] * 6,
        out_specs=(VMEM, VMEM),
        scratch_shapes=[
            pltpu.VMEM((2, TILES, K, 8, 128), F32),
            pltpu.VMEM((2, 3, 8, TILES * 128), F32),
            pltpu.VMEM((2, 8, TILES * 128), F32),
            pltpu.VMEM((ROWS, COLS), jnp.int32),
            pltpu.VMEM((1, 1, SENS), jnp.int32),
            pltpu.VMEM((2, 3, 1, 1, SENS), F32),
            pltpu.VMEM((16, TILES * 128), F32),
            pltpu.SemaphoreType.DMA((3, TILES + 2)),
        ],
        compiler_params=pltpu.CompilerParams(vmem_limit_bytes=8 * MB),
        name="pack_x",
    )(adjoint, velocity, density, heights, cells, misfit)


def place_x(message, side, slot, tile, field, u, force):
    outer, inner = (BASE + ROWS, BASE + ROWS + 1) if side == "lo" else (BASE - 1, BASE - 2)
    flat = field.reshape(field.shape[0], K * EXT, 128)
    at = pl.ds(tile * 128, 128)
    flat[slot, pl.ds(outer, 8, stride=EXT), :] = message[0:8, at]
    flat[slot, pl.ds(8 * EXT + outer, 8, stride=EXT), :] = message[8:16, at]
    flat[slot, pl.ds(16 * EXT + outer, 3, stride=EXT), :] = message[16:19, at]
    for index, number in enumerate(X_SIDE[side]):
        field[slot, number, inner : inner + 1, :] = message[19 + index : 20 + index, at]
    for axis in range(3):
        force[slot, 1, axis, outer : outer + 1, :] = message[24 + axis : 25 + axis, at]
        u[slot, 1, axis, outer : outer + 1, :] = message[27 + axis : 28 + axis, at]


def place_tall(message, side, tall):
    outer, inner = (BASE + ROWS, BASE + ROWS + 1) if side == "lo" else (BASE - 1, BASE - 2)
    tall[outer : outer + 1, 0:COLS] = message[30:31, 0:COLS]
    tall[inner : inner + 1, 0:COLS] = message[30:31, 128 : 128 + COLS]


def column_tops(tall, tile, rows):
    at = slice(rows, rows + 8)
    low = lanes() < NZ
    left = jnp.broadcast_to(tall[at, 2 * tile : 2 * tile + 1], (8, 128))
    right = jnp.broadcast_to(tall[at, 2 * tile + 1 : 2 * tile + 2], (8, 128))
    return jnp.where(low, left, right)


def shifted_tops(geo, tops, tile, rows):
    at = pl.ds(rows, 8)
    after, before = (tile + 1) % (TILES + 1), (tile - 1) % (TILES + 1)
    here = tops[0, tile, at, :]
    tops[1, tile, at, :] = half_turn(from_next(geo, here, tops[0, after, at, :]))
    tops[2, tile, at, :] = half_turn(from_previous(geo, here, tops[0, before, at, :]))


def step(geo, number_of_step, source, target, u, force, tops, starts, tile, after, before):
    def read(where, number, row):
        return source[where, number, pl.ds(row, 8), :]

    def top(cy, row):
        return tops[cy % 3, tile, pl.ds(row, 8), :]

    for start in starts:
        at = pl.ds(start, 8)
        f = incoming(geo, read, top, tile, after, before, start, range(K))
        velocity = [u[tile, number_of_step, axis, at, :] for axis in range(3)]
        push = [force[tile, number_of_step, axis, at, :] for axis in range(3)]
        result = collide(f, velocity, push, range(K), number_of_step)
        if number_of_step:
            for number in range(K):
                target[tile, number, at, :] = result[number]
        else:
            fluid = geo.level >= tops[0, tile, at, :]
            for number in range(K):
                target[tile, number, at, :] = jnp.zeros((8, 128), F32)
                pltpu.store(target.at[tile, number, at, :], result[number], mask=fluid)


WIDE = TILES + 1
SENT_EARLY = 10
FIELD = jax.ShapeDtypeStruct((WIDE, K, EXT, 128), F32)
VECTORS = jax.ShapeDtypeStruct((TILES, 2, 3, EXT, 128), F32)
TOPS = jax.ShapeDtypeStruct((3, WIDE, EXT, 128), F32)
TALL = jax.ShapeDtypeStruct((EXT, 128), F32)


def prepare_kernel(adjoint, velocity, density, heights_hbm, cells_hbm, misfit_hbm,
                   field, middle, u, force, tops, tall, rho, heights, cells, misfit, sems):
    own = pl.ds(BASE, ROWS)
    small = [
        pltpu.make_async_copy(heights_hbm, heights, sems.at[2, 1]),
        pltpu.make_async_copy(cells_hbm, cells, sems.at[2, 2]),
        pltpu.make_async_copy(misfit_hbm, misfit, sems.at[2, 3]),
    ]
    for copy in small:
        copy.start()
    load_rho = pltpu.make_async_copy(density, rho, sems.at[2, 0])
    load_rho.start()

    def load(tile):
        at = pl.ds(pl.multiple_of(tile * 128, 128), 128)
        return (
            pltpu.make_async_copy(adjoint.at[:, :, at], field.at[tile, :, own, :], sems.at[0, tile]),
            pltpu.make_async_copy(velocity.at[:, :, :, at], u.at[tile, :, :, own, :], sems.at[1, tile]),
        )

    def arrived(tile):
        for copy in load(tile):
            copy.wait()

    for tile in range(TILES):
        for copy in load(tile):
            copy.start()
    geo = Geometry()
    for copy in small:
        copy.wait()
    tall[BASE : BASE + ROWS, 0:COLS] = heights[...].astype(F32)
    for tile in range(TILES):
        for row in range(BASE, BASE + ROWS, 8):
            tops[0, tile, row : row + 8] = column_tops(tall, tile, row)
    for tile in range(1, TILES - 1):
        for row in range(BASE, BASE + ROWS, 8):
            shifted_tops(geo, tops, tile, row)

    numbers = cells[0]
    row = numbers // (COLS * NZ)
    lane = numbers % (COLS * NZ)
    here = lax.broadcasted_iota(jnp.int32, (ROWS, SENS), 0) == row
    parts = []
    for back in range(2):
        for axis in range(3):
            parts.append(split(jnp.where(here, SCALES[back][1] * misfit[back, axis, 0], 0.0)))
    left = jnp.concatenate(
        [jnp.concatenate([part[index] for part in parts], axis=0) for index in range(2)], axis=1
    )
    load_rho.wait()
    for pair in range(TILES // 2):
        right = one_hot(lane, 2 * pair, 256)
        summed = product(left, jnp.concatenate([right, right], axis=1))
        for half in range(2):
            tile = 2 * pair + half
            at = pl.ds(tile * 128, 128)
            for back in range(2):
                inverse = 1.0 / rho[back, :, at]
                for axis in range(3):
                    first = (3 * back + axis) * ROWS
                    force[tile, back, axis, own, :] = (
                        summed[first : first + ROWS, 128 * half : 128 * half + 128] * inverse
                    )
    arrived(0)
    arrived(1)

    def inner(tile, carry):
        arrived(tile + 1)
        step(geo, 1, field, middle, u, force, tops, STARTS_INNER, tile, tile + 1, tile - 1)
        return carry

    lax.fori_loop(1, TILES - 1, inner, 0)


def prepare(adjoint, velocity, density, heights, cells, misfit):
    return pl.pallas_call(
        prepare_kernel,
        out_shape=(FIELD, FIELD, VECTORS, VECTORS, TOPS, TALL),
        in_specs=[HBM] * 6,
        out_specs=(VMEM,) * 6,
        scratch_shapes=[
            pltpu.VMEM((2, ROWS, TILES * 128), F32),
            pltpu.VMEM((ROWS, COLS), jnp.int32),
            pltpu.VMEM((1, 1, SENS), jnp.int32),
            pltpu.VMEM((2, 3, 1, 1, SENS), F32),
            pltpu.SemaphoreType.DMA((3, TILES)),
        ],
        compiler_params=pltpu.CompilerParams(vmem_limit_bytes=PREPARE_VMEM),
        cost_estimate=pl.CostEstimate(flops=40_000_000, bytes_accessed=8_000_000, transcendentals=0),
        name="prepare",
    )(adjoint, velocity, density, heights, cells, misfit)


def pack_y_kernel(own_tall, all_field, all_u, all_force, msg_a, msg_b,
                  out_a, out_b, field, u, force, tall, tops, partial):
    slots = ((0, 0), (1, TILES - 1))
    own = pl.ds(BASE, ROWS)
    for slot, tile in slots:
        field[slot, :, own, :] = all_field[tile, :, own, :]
        u[slot, 1, :, own, :] = all_u[tile, 1, :, own, :]
        force[slot, 1, :, own, :] = all_force[tile, 1, :, own, :]
    tall[BASE : BASE + ROWS] = own_tall[BASE : BASE + ROWS]
    geo = Geometry()

    def from_x(low_msg, high_msg):
        for message, side in ((low_msg, "lo"), (high_msg, "hi")):
            place_tall(message, side, tall)
            for slot, tile in slots:
                place_x(message, side, slot, tile, field, u, force)

    by_parity(1 - lax.axis_index("gx") % 2, lambda: from_x(msg_a, msg_b), lambda: from_x(msg_b, msg_a))
    for slot, tile in slots:
        for row in range(0, EXT, 8):
            value = column_tops(tall, tile, row)
            tops[slot, 0, row : row + 8] = value
            tops[slot, 1, row : row + 8] = half_turn(value)

    def read(tile, number, row):
        return field[tile, number, pl.ds(row, 8), :]

    for slot, side in ((0, "lo"), (1, "hi")):
        inward = 1 if side == "lo" else -1
        numbers = [n for n in range(K) if VELOCITIES[n][1] in (0, inward)]
        for start in STARTS_WIDE:
            at = pl.ds(start, 8)

            def top(cy, row, slot=slot):
                return tops[slot, 0 if cy == 0 else 1, pl.ds(row, 8), :]

            f = incoming(geo, read, top, slot, slot, slot, start, numbers)
            velocity_here = [u[slot, 1, axis, at, :] for axis in range(3)]
            push = [force[slot, 1, axis, at, :] for axis in range(3)]
            result = collide(f, velocity_here, push, Y_SIDE[side], 1)
            for index, number in enumerate(Y_SIDE[side]):
                partial[slot, index, at, :] = result[number]

    def write(side, out):
        slot = 0 if side == "lo" else 1
        for start in range(0, 40, 8):
            at = pl.ds(start + BASE - 2, 8)
            pairs = [
                (field[slot, number, at, :], partial[slot, index, at, :])
                for index, number in enumerate(Y_SIDE[side])
            ]
            pairs.append((u[slot, 1, 0, at, :], u[slot, 1, 1, at, :]))
            pairs.append((u[slot, 1, 2, at, :], tops[slot, 0, at, :]))
            for index, (first, second) in enumerate(pairs):
                turned = half_turn(second)
                if side == "lo":
                    value = jnp.where(geo.low, first, turned)
                else:
                    value = jnp.where(geo.low, turned, first)
                out[index, start : start + 8, :] = value

    def upper():
        write("hi", out_a)
        write("lo", out_b)

    def lower():
        write("lo", out_a)
        write("hi", out_b)

    by_parity(lax.axis_index("gy") % 2, upper, lower)


def pack_y(heights, field, u, force, msg_a, msg_b):
    shape = jax.ShapeDtypeStruct((Y_FIELDS, 40, 128), F32)
    return pl.pallas_call(
        pack_y_kernel,
        out_shape=(shape, shape),
        in_specs=[VMEM] * 6,
        out_specs=(VMEM, VMEM),
        scratch_shapes=[
            pltpu.VMEM((2, K, EXT, 128), F32),
            pltpu.VMEM((2, 2, 3, EXT, 128), F32),
            pltpu.VMEM((2, 2, 3, EXT, 128), F32),
            pltpu.VMEM((EXT, 128), F32),
            pltpu.VMEM((2, 2, EXT, 128), F32),
            pltpu.VMEM((2, 5, EXT, 128), F32),
        ],
        compiler_params=pltpu.CompilerParams(vmem_limit_bytes=SMALL_VMEM),
        name="pack_y",
    )(heights, field, u, force, msg_a, msg_b)


def send_out(field, out, sems, tile):
    at = pl.ds(pl.multiple_of(tile * 128, 128), 128)
    return pltpu.make_async_copy(field.at[tile, :, pl.ds(BASE, ROWS), :], out.at[:, :, at], sems.at[tile])


def inner_kernel(own_tall, msg_a, msg_b, order, field_in, middle_in, u_in, force_in, tops_in,
                 field, middle, u, force, tops, out, tall, sems):
    del order, field_in, middle_in, u_in, force_in, tops_in
    geo = Geometry()
    tall[BASE : BASE + ROWS] = own_tall[BASE : BASE + ROWS]

    def from_x(low_msg, high_msg):
        for message, side in ((low_msg, "lo"), (high_msg, "hi")):
            place_tall(message, side, tall)
            for tile in range(TILES):
                place_x(message, side, tile, tile, field, u, force)

    by_parity(1 - lax.axis_index("gx") % 2, lambda: from_x(msg_a, msg_b), lambda: from_x(msg_b, msg_a))
    for tile in range(TILES):
        for row in (0, BASE + ROWS):
            tops[0, tile, row : row + 8] = column_tops(tall, tile, row)
    for tile in range(1, TILES - 1):
        for row in (0, BASE + ROWS):
            shifted_tops(geo, tops, tile, row)

    def edges(tile):
        step(geo, 1, field, middle, u, force, tops, STARTS_EDGE, tile, tile + 1, tile - 1)

    edges(1)
    edges(2)

    def second(tile, carry):
        edges(tile + 1)
        step(geo, 0, middle, field, u, force, tops, STARTS_OWN, tile, tile + 1, tile - 1)
        pl.when(tile < SENT_EARLY)(lambda: send_out(field, out, sems, tile).start())
        return carry

    def sent(tile, carry):
        send_out(field, out, sems, tile).wait()
        return carry

    lax.fori_loop(2, TILES - 2, second, 0)
    lax.fori_loop(2, SENT_EARLY, sent, 0)


def inner_columns(heights, msg_a, msg_b, order, field, middle, u, force, tops, shape):
    return pl.pallas_call(
        inner_kernel,
        out_shape=(FIELD, FIELD, VECTORS, VECTORS, TOPS, jax.ShapeDtypeStruct(shape, F32)),
        in_specs=[VMEM] * 3 + [HBM] + [VMEM] * 5,
        out_specs=(VMEM,) * 5 + (HBM,),
        input_output_aliases={4: 0, 5: 1, 6: 2, 7: 3, 8: 4},
        scratch_shapes=[pltpu.VMEM((EXT, 128), F32), pltpu.SemaphoreType.DMA((TILES,))],
        compiler_params=pltpu.CompilerParams(vmem_limit_bytes=SMALL_VMEM),
        cost_estimate=pl.CostEstimate(flops=40_000_000, bytes_accessed=8_000_000, transcendentals=0),
        name="inner_columns",
    )(heights, msg_a, msg_b, order, field, middle, u, force, tops)


def outer_kernel(msg_a, msg_b, field_in, middle_in, u, force, tops_in, out_in,
                 field, middle, tops, out, side_partial, side_u, sems):
    del field_in, middle_in, tops_in, out_in
    for tile in range(SENT_EARLY, TILES - 2):
        send_out(field, out, sems, tile).start()
    geo = Geometry()

    def from_y(low_msg, high_msg):
        for start in range(0, 40, 8):
            at = pl.ds(start + BASE - 2, 8)
            for index in range(Y_FIELDS):
                low_value = low_msg[index, start : start + 8, :]
                high_value = high_msg[index, start : start + 8, :]
                low_turned, high_turned = half_turn(low_value), half_turn(high_value)
                if index < 5:
                    field[TILES, Y_SIDE["lo"][index], at, :] = low_value
                    field[TILES, Y_SIDE["hi"][index], at, :] = high_value
                    side_partial[0, index, at, :] = low_turned
                    side_partial[1, index, at, :] = high_turned
                else:
                    first = jnp.where(geo.low, low_value, high_value)
                    second = jnp.where(geo.low, low_turned, high_turned)
                    if index == 5:
                        side_u[0, at, :] = first
                        side_u[1, at, :] = second
                    else:
                        side_u[2, at, :] = first
                        tops[0, TILES, at, :] = second

    by_parity(lax.axis_index("gy") % 2, lambda: from_y(msg_a, msg_b), lambda: from_y(msg_b, msg_a))
    for tile in (0, TILES - 1, TILES):
        for row in range(0, EXT, 8):
            shifted_tops(geo, tops, tile, row)
    for tile, after, before in ((0, 1, TILES), (TILES - 1, TILES, TILES - 2)):
        step(geo, 1, field, middle, u, force, tops, STARTS_WIDE, tile, after, before)

    def read(where, number, row):
        return field[where, number, pl.ds(row, 8), :]

    def top(cy, row):
        return tops[cy % 3, TILES, pl.ds(row, 8), :]

    for slot, side, other in ((0, "lo", "hi"), (1, "hi", "lo")):
        for start in STARTS_WIDE:
            at = pl.ds(start, 8)
            f = incoming(geo, read, top, TILES, 0, TILES - 1, start, Y_SIDE[other])
            velocity = [side_u[axis, at, :] for axis in range(3)]
            result = collide(f, velocity, None, Y_SIDE[side], 1)
            for index, number in enumerate(Y_SIDE[side]):
                middle[TILES, number, at, :] = result[number] + side_partial[slot, index, at, :]

    last = (1, TILES - 2, 0, TILES - 1)
    for tile in last:
        before = TILES if tile == 0 else tile - 1
        step(geo, 0, middle, field, u, force, tops, STARTS_OWN, tile, tile + 1, before)
        send_out(field, out, sems, tile).start()
    for tile in tuple(range(SENT_EARLY, TILES - 2)) + last:
        send_out(field, out, sems, tile).wait()


def outer_columns(msg_a, msg_b, field, middle, u, force, tops, out):
    return pl.pallas_call(
        outer_kernel,
        out_shape=(FIELD, FIELD, TOPS, jax.ShapeDtypeStruct(out.shape, F32)),
        in_specs=[VMEM] * 7 + [HBM],
        out_specs=(VMEM,) * 3 + (HBM,),
        input_output_aliases={2: 0, 3: 1, 6: 2, 7: 3},
        scratch_shapes=[
            pltpu.VMEM((2, 5, EXT, 128), F32),
            pltpu.VMEM((3, EXT, 128), F32),
            pltpu.SemaphoreType.DMA((TILES,)),
        ],
        compiler_params=pltpu.CompilerParams(vmem_limit_bytes=SMALL_VMEM),
        name="outer_columns",
    )(msg_a, msg_b, field, middle, u, force, tops, out)


def partners(count, odd):
    if not odd:
        return [(i, i ^ 1) for i in range(count)]
    return [(i, (i - 1) % count if i % 2 == 0 else (i + 1) % count) for i in range(count)]


def swap(value, axis, odd):
    return lax.ppermute(value, axis, partners(lax.axis_size(axis), odd))


def per_device(adjoint, velocity, density, heights, cells, misfit):
    args = [
        pltpu.with_memory_space_constraint(value, pltpu.HBM)
        for value in (adjoint, velocity, density, heights, cells, misfit)
    ]
    x_a, x_b = pack_x(*args)
    x_a, x_b = swap(x_a, "gx", False), swap(x_b, "gx", True)
    field, middle, u, force, tops, tall = prepare(*args)
    own_a, own_b = pack_y(tall, field, u, force, x_a, x_b)
    y_a, y_b = swap(own_a, "gy", True), swap(own_b, "gy", False)
    field, middle, u, force, tops, out = inner_columns(
        tall, x_a, x_b, own_a, field, middle, u, force, tops, adjoint.shape
    )
    return outer_columns(y_a, y_b, field, middle, u, force, tops, out)[3]


def solution(mesh):
    return jax.shard_map(
        per_device,
        mesh=mesh,
        in_specs=(
            P(None, "gx", "gy"),
            P(None, None, "gx", "gy"),
            P(None, "gx", "gy"),
            P("gx", "gy"),
            P("gx", "gy", None),
            P(None, None, "gx", "gy", None),
        ),
        out_specs=P(None, "gx", "gy"),
        check_vma=False,
    )
```
